256 devices in a mesh: dom: 64 (over x, z, core), col: 4 (over y).
Axes of the slice: x: 4, y: 4, z: 8, core: 2. Of those that a mesh axis runs over, the one named last changes fastest.
Arguments:
- embeddings: float32 [262144, 512], P('dom', 'col'), may hold values from -1.3 to 1.3
- adagrad_state: float32 [262144], P('dom'), may hold values from 1e-05 to 0.01
- relations: float32 [1345, 512], P(None, 'col'), may hold values from 0.1 to 1.9
- src_rows: int32 [262144], P('dom'), may hold values from 0 to 4095
- dst_rows: int32 [262144], P('dom'), may hold values from 0 to 4095
- rel_ids: int32 [262144], P('dom'), may hold values from 0 to 1344
- bucket_counts: int32 [64, 64], P('dom'), may hold values from 1 to 64, as said below
- neg_rows: int32 [64000], P('dom'), may hold values from 0 to 4095
Outputs:
- new_embeddings: float32 [262144, 512], P('dom', 'col')
- new_state: float32 [262144], P('dom')
The draws below stay inside these ranges and needn't reach their ends.
Inputs may be any that keep to these rules, and one draw needn't show every extreme that they name: `bucket_counts`: edge slot j of a partition lies in the bucket of destination partition j // 64; in every draw some destination partition has all 64 slots live from every source partition.
All inputs are finite; a program needn't handle non-finite values.
Results may differ from the reference program's by a relative error of at most 0.0025.
Values may be sent and summed in bfloat16 or wider, within the bound.
No kernel may reach another device: no remote copies, remote signals or barrier semaphores. Data moves between devices by JAX's collectives and lax.ppermute only.
A program may use at most 128 MiB of HBM per device.

```python
import math
import jax
import jax.numpy as jnp
import numpy as np
from jax import lax

D = 512
RELS = 1345
ENT_DEV = 4096
EDGE_SLOTS = 4096
NEG = 1000
ENTITIES = 262144
ALL_SLOTS = 262144
ALL_NEG = 64000
N_DOM = 64


def draw_bucket_counts(key, part):
    key = jax.random.fold_in(key, 7)
    first_key, second_key = jax.random.split(key)
    per_owner = EDGE_SLOTS // N_DOM
    uneven = jax.random.randint(first_key, (N_DOM, N_DOM), 1, per_owner + 1)
    hottest = jax.random.randint(second_key, (), 0, N_DOM)
    column_ids = jnp.arange(N_DOM, dtype=jnp.int32)[None, :]
    return jnp.where(column_ids == hottest, per_owner, uneven).astype(jnp.int32)


def plant(values, own_key, low, high):
    longest = values.shape.index(max(values.shape))
    spots = []
    for shift in (0, 1):
        where = [jax.random.randint(jax.random.fold_in(own_key, axis), (), 0, length) for axis, length in enumerate(values.shape)]
        where[longest] = (where[longest] + shift) % values.shape[longest]
        spots.append(tuple(where))
    return values.at[spots[0]].set(low).at[spots[1]].set(high)


def block_levels(own_key, shape, pieces, low, high):
    factor_of = 1.0
    for axis_at, parts in pieces:
        draws = jax.random.uniform(jax.random.fold_in(jax.random.fold_in(own_key, 6), axis_at), (parts,), jnp.float32, low / len(pieces), high / len(pieces))
        factor_of = factor_of * jnp.repeat(jnp.exp(draws), shape[axis_at] // parts).reshape((-1,) + (1,) * (len(shape) - 1 - axis_at))
    return factor_of


def rank_table(number_of, slope):
    weights = [(1 << 20) // math.isqrt(standing ** slope) + 1 for standing in range(1, number_of + 1)]
    scale = 1 + sum(weights) // (1 << 30)
    return np.cumsum(np.array([max(1, weight // scale) for weight in weights]))


def ranked_ids(stream_key, extent, amount, skew):
    table = rank_table(amount, skew)
    pick = jax.random.randint(jax.random.fold_in(stream_key, 1), extent, 0, int(table[amount - 1]))
    grade = jnp.searchsorted(jnp.asarray(table, jnp.int32), pick, side="right")
    return jax.random.permutation(jax.random.fold_in(stream_key, 2), amount)[grade].astype(jnp.int32)


def scatter_about(key, shape, spread, most, cuts=(), kind=jnp.bfloat16):
    entries = jax.random.normal(key, shape, jnp.float32) * spread
    if len(cuts) > 0:
        entries = block_levels(key, shape, cuts, -0.22, 0.18) * entries
    return jnp.clip(entries, min=-most, max=most).astype(kind)


def setup_inputs(seed: int = 0) -> dict:
    streams_of = jax.random.split(jax.random.key(seed), 9)
    embeddings = scatter_about(streams_of[0], (ENTITIES, D), 0.21, 1.3, ((0, 64), (1, 4)), jnp.float32)
    adagrad_state = jnp.clip(jnp.exp(math.log(0.01) - 6.9077553 * jax.random.uniform(streams_of[1], (ENTITIES,), jnp.float32) ** block_levels(streams_of[1], (ENTITIES,), ((0, 64),), -0.2, 0.2)), 9.999999747378752e-06, 0.01)
    relations = jnp.clip(1.0 + 0.18 * jax.random.normal(streams_of[2], (RELS, D), jnp.float32), 0.1, 1.9)
    src_rows = plant(ranked_ids(streams_of[3], (ALL_SLOTS,), ENT_DEV, 2), jax.random.fold_in(streams_of[3], 3), 0, ENT_DEV - 1).astype(jnp.int32)
    dst_rows = plant(ranked_ids(streams_of[4], (ALL_SLOTS,), ENT_DEV, 2), jax.random.fold_in(streams_of[4], 3), 0, ENT_DEV - 1).astype(jnp.int32)
    rel_ids = plant(ranked_ids(streams_of[5], (ALL_SLOTS,), RELS, 2), jax.random.fold_in(streams_of[5], 3), 0, RELS - 1).astype(jnp.int32)
    bucket_counts = draw_bucket_counts(jax.random.fold_in(streams_of[8], 71), 0)
    neg_rows = plant(jax.random.randint(streams_of[7], (ALL_NEG,), 0, ENT_DEV), jax.random.fold_in(streams_of[7], 1), 0, ENT_DEV - 1).astype(jnp.int32)
    return {"embeddings": embeddings, "adagrad_state": adagrad_state, "relations": relations, "src_rows": src_rows, "dst_rows": dst_rows, "rel_ids": rel_ids, "bucket_counts": bucket_counts, "neg_rows": neg_rows}


learning_rate = 0.3

def reference(embeddings, adagrad_state, relations, src_rows, dst_rows, rel_ids, bucket_counts, neg_rows):
    per_owner = EDGE_SLOTS // N_DOM
    slot_ids = jnp.arange(EDGE_SLOTS, dtype=jnp.int32)
    owner_of_slot = slot_ids // per_owner

    def one_device(running, device_index):
        first_row = device_index * ENT_DEV
        source = lax.dynamic_slice_in_dim(src_rows, device_index * EDGE_SLOTS, EDGE_SLOTS) + first_row
        target = lax.dynamic_slice_in_dim(dst_rows, device_index * EDGE_SLOTS, EDGE_SLOTS) + owner_of_slot * ENT_DEV
        relation_ids = lax.dynamic_slice_in_dim(rel_ids, device_index * EDGE_SLOTS, EDGE_SLOTS)
        negative = lax.dynamic_slice_in_dim(neg_rows, device_index * NEG, NEG) + first_row
        counts = lax.dynamic_index_in_dim(bucket_counts, device_index, 0, keepdims=False)
        live = (slot_ids % per_owner < counts[owner_of_slot]).astype(jnp.float32)
        head_rows = embeddings[source].astype(jnp.bfloat16)
        tail_rows = embeddings[target].astype(jnp.bfloat16)
        corrupt_rows = embeddings[negative].astype(jnp.bfloat16)
        relation = relations[relation_ids]
        weighted = (relation * tail_rows.astype(jnp.float32)).astype(jnp.bfloat16)
        positive = lax.optimization_barrier(jnp.sum(head_rows.astype(jnp.float32) * weighted.astype(jnp.float32), axis=1))
        scores = jnp.dot(corrupt_rows, weighted.T, preferred_element_type=jnp.float32)
        grad_positive = -live * jax.nn.sigmoid(-positive)
        grad_scores = (live[None, :] * jax.nn.sigmoid(scores) / NEG).astype(jnp.bfloat16)
        grad_head = grad_positive[:, None] * weighted.astype(jnp.float32)
        pulled = jnp.dot(grad_scores.T, corrupt_rows, preferred_element_type=jnp.float32)
        grad_tail = grad_positive[:, None] * head_rows.astype(jnp.float32) * relation + relation * pulled
        grad_corrupt = jnp.dot(grad_scores, weighted, preferred_element_type=jnp.float32)
        running = running.at[source].add(grad_head).at[target].add(grad_tail).at[negative].add(grad_corrupt)
        return (running, None)
    gradient, _ = lax.scan(one_device, jnp.zeros(embeddings.shape, jnp.float32), jnp.arange(N_DOM, dtype=jnp.int32))
    new_state = adagrad_state + lax.optimization_barrier(jnp.mean(gradient * gradient, axis=1))
    new_embeddings = embeddings - learning_rate * gradient / jnp.sqrt(new_state)[:, None]
    return (new_embeddings, new_state)
```

```python
import functools
import jax
import jax.numpy as jnp
from jax import lax
from jax.experimental import pallas as pl
from jax.experimental.pallas import tpu as pltpu
from jax.sharding import PartitionSpec as P

learning_rate = 0.3
OWNERS = 64
COLS = 4
PART = 16
SLOTS = OWNERS * COLS * PART
EDGES = OWNERS * PART
WIDTH = 128
NEG = 1000
NEG_PAD = 1008
PIECE = EDGES + NEG_PAD
ROW_BITS = 12
CHAINS = 4

F32, BF16 = jnp.float32, jnp.bfloat16
SMEM = pl.BlockSpec(memory_space=pltpu.SMEM)
VMEM = pl.BlockSpec(memory_space=pltpu.VMEM)


def call(body, name, out, ins, scratch, flops=0, moved=0):
    return pl.pallas_call(
        body,
        out_shape=out,
        in_specs=ins,
        out_specs=jax.tree.map(lambda _: VMEM, out),
        scratch_shapes=scratch,
        compiler_params=pltpu.CompilerParams(vmem_limit_bytes=40 * 1024 * 1024),
        cost_estimate=pl.CostEstimate(flops=flops, bytes_accessed=moved, transcendentals=0),
        name=name,
    )


def shape(rows, dtype):
    return jax.ShapeDtypeStruct((rows, WIDTH), dtype)


def gather_heads_body(col, src, neg, table, *rest):
    outs, (rows, corrupt) = rest[:COLS], rest[COLS:]
    for s in range(COLS):
        quarter = (col[0] + s) & (COLS - 1)

        @pl.loop(0, OWNERS)
        def _(b):
            base = (b * COLS + quarter) * PART
            for i in range(PART):
                rows[pl.ds(s * EDGES + b * PART + i, 1), :] = table[pl.ds(src[base + i], 1), :]

    @pl.loop(0, NEG // 8)
    def _(g):
        for i in range(8):
            corrupt[pl.ds(g * 8 + i, 1), :] = table[pl.ds(neg[g * 8 + i], 1), :]

    corrupt[NEG:NEG_PAD, :] = jnp.zeros((NEG_PAD - NEG, WIDTH), F32)
    rounded = corrupt[...].astype(BF16)
    for s in range(COLS):
        outs[s][0:EDGES, :] = rows[s * EDGES : (s + 1) * EDGES, :].astype(BF16)
        outs[s][EDGES:PIECE, :] = rounded


def gather_heads(col, src, neg, table):
    return call(
        gather_heads_body,
        "gather_heads",
        [shape(PIECE, BF16)] * COLS,
        [SMEM, SMEM, SMEM, VMEM],
        [pltpu.VMEM((SLOTS, WIDTH), F32), pltpu.VMEM((NEG_PAD, WIDTH), F32)],
        moved=20_000_000,
    )(col, src, neg, table)


def gather_tails_body(wanted, table, relations, weighted, factors, rows):
    @pl.loop(0, SLOTS // 16)
    def _(g):
        for i in range(16):
            j = g * 16 + i
            word = wanted[j]
            rows[pl.ds(j, 1), :] = table[pl.ds(word & ((1 << ROW_BITS) - 1), 1), :]
            factors[pl.ds(j, 1), :] = relations[pl.ds(word >> ROW_BITS, 1), :]

    weighted[...] = (factors[...] * rows[...].astype(BF16).astype(F32)).astype(BF16)


def gather_tails(wanted, table, relations):
    return call(
        gather_tails_body,
        "gather_tails",
        [shape(SLOTS, BF16), shape(SLOTS, F32)],
        [SMEM, VMEM, VMEM],
        [pltpu.VMEM((SLOTS, WIDTH), F32)],
        moved=20_000_000,
    )(wanted, table, relations)


def edge_scores_body(col, weighted, live, p0, p1, p2, p3, pulled_out, o0, o1, o2, o3, w, heads, corrupt):
    outs = (o0, o1, o2, o3)
    owner = [(col[0] + COLS - s) & (COLS - 1) for s in range(COLS)]
    span = [slice(s * WIDTH, (s + 1) * WIDTH) for s in range(COLS)]
    for s, piece in enumerate((p0, p1, p2, p3)):
        w[:, span[s]] = weighted[:, owner[s]].reshape(EDGES, WIDTH)
        heads[:, span[s]] = piece[0:EDGES, :]
        corrupt[0:NEG_PAD, span[s]] = piece[EDGES:PIECE, :]
        corrupt[NEG_PAD:1024, span[s]] = jnp.zeros((1024 - NEG_PAD, WIDTH), BF16)
    grad_corrupt = jnp.zeros((1024, COLS * WIDTH), F32)
    negatives = corrupt[...]
    block = 256
    for k in range(EDGES // block):
        rows = slice(k * block, (k + 1) * block)
        wk = w[rows, :]
        wf = wk.astype(F32)
        hf = heads[rows, :].astype(F32)
        mask = live[rows, :]
        positive = jnp.sum(hf * wf, axis=1, keepdims=True)
        grad_positive = -mask * jax.nn.sigmoid(-positive)
        scores = lax.dot_general(wk, negatives, (((1,), (1,)), ((), ())), preferred_element_type=F32)
        grad_scores = (mask * jax.nn.sigmoid(scores) * (1.0 / NEG)).astype(BF16)
        pulled = jnp.dot(grad_scores, negatives, preferred_element_type=F32)
        pulled = (grad_positive * hf + pulled).astype(BF16)
        grad_head = (grad_positive * wf).astype(BF16)
        grad_corrupt += lax.dot_general(
            grad_scores, wk, (((0,), (0,)), ((), ())), preferred_element_type=F32
        )
        for s in range(COLS):
            buckets = block // PART
            pulled_out[pl.ds(k * buckets, buckets), owner[s]] = pulled[:, span[s]].reshape(
                buckets, PART, WIDTH
            )
            outs[s][rows, :] = grad_head[:, span[s]]
    for s in range(COLS):
        outs[s][EDGES:PIECE, :] = grad_corrupt[0:NEG_PAD, span[s]].astype(BF16)


def edge_scores(col, weighted, live, pieces):
    return call(
        edge_scores_body,
        "edge_scores",
        [jax.ShapeDtypeStruct((OWNERS, COLS, PART, WIDTH), BF16)] + [shape(PIECE, BF16)] * COLS,
        [SMEM] + [VMEM] * 6,
        [pltpu.VMEM((EDGES, COLS * WIDTH), BF16)] * 2 + [pltpu.VMEM((1024, COLS * WIDTH), BF16)],
        flops=3_200_000_000,
        moved=5_000_000,
    )(col, weighted, live, *pieces)


def total_of(tables):
    total = tables[0][...]
    for table in tables[1:]:
        total += table[...]
    return total


def scatter_heads_body(col, src, neg, g0, g1, g2, g3, out, rows, corrupt, *tables):
    tables = (out,) + tables
    for table in tables:
        table[...] = jnp.zeros((SLOTS, WIDTH), F32)
    grad_corrupt = jnp.zeros((NEG_PAD, WIDTH), F32)
    for s, piece in enumerate((g0, g1, g2, g3)):
        rows[s * EDGES : (s + 1) * EDGES, :] = piece[0:EDGES, :].astype(F32)
        grad_corrupt += piece[EDGES:PIECE, :].astype(F32)
    corrupt[...] = grad_corrupt
    for s in range(COLS):
        quarter = (col[0] + s) & (COLS - 1)

        @pl.loop(0, OWNERS)
        def _(b):
            base = (b * COLS + quarter) * PART
            for i in range(PART):
                into = tables[i % CHAINS]
                into[pl.ds(src[base + i], 1), :] += rows[pl.ds(s * EDGES + b * PART + i, 1), :]

    @pl.loop(0, NEG // 8)
    def _(g):
        for i in range(8):
            into = tables[i % CHAINS]
            into[pl.ds(neg[g * 8 + i], 1), :] += corrupt[pl.ds(g * 8 + i, 1), :]

    out[...] = total_of(tables)


def scatter_heads(col, src, neg, pieces):
    return call(
        scatter_heads_body,
        "scatter_heads",
        shape(SLOTS, F32),
        [SMEM] * 3 + [VMEM] * 4,
        [pltpu.VMEM((SLOTS, WIDTH), F32), pltpu.VMEM((NEG_PAD, WIDTH), F32)]
        + [pltpu.VMEM((SLOTS, WIDTH), F32)] * (CHAINS - 1),
        moved=30_000_000,
    )(col, src, neg, *pieces)


def scatter_tails_body(wanted, start, factors, pulled, out, rows, *tables):
    tables = (out,) + tables
    out[...] = start[...]
    for table in tables[1:]:
        table[...] = jnp.zeros((SLOTS, WIDTH), F32)
    rows[...] = factors[...] * pulled[...].astype(F32)

    @pl.loop(0, SLOTS // 16)
    def _(g):
        for i in range(16):
            j = g * 16 + i
            into = tables[i % CHAINS]
            into[pl.ds(wanted[j] & ((1 << ROW_BITS) - 1), 1), :] += rows[pl.ds(j, 1), :]

    out[...] = total_of(tables)


def scatter_tails(wanted, start, factors, pulled):
    return call(
        scatter_tails_body,
        "scatter_tails",
        shape(SLOTS, F32),
        [SMEM] + [VMEM] * 3,
        [pltpu.VMEM((SLOTS, WIDTH), F32)] * CHAINS,
        moved=30_000_000,
    )(wanted, start, factors, pulled)


def shifted(x, s):
    return lax.ppermute(x, "col", [(i, (i + s) % COLS) for i in range(COLS)])


def shards(
    embeddings, adagrad_state, relations, src_rows, dst_rows, rel_ids, bucket_counts, neg_rows
):
    axes = ("dom", "col")
    me = lax.axis_index("col")
    col = me.astype(jnp.int32).reshape(1)
    first = lax.broadcasted_iota(jnp.int32, (OWNERS, PART), 1) + me * PART
    live = (first < bucket_counts[0][:, None]).astype(F32).reshape(EDGES, 1)

    words = dst_rows | (rel_ids << ROW_BITS)
    wanted = lax.all_to_all(
        words.reshape(OWNERS, SLOTS // OWNERS), "dom", split_axis=0, concat_axis=0, tiled=True
    ).reshape(SLOTS)
    pieces = gather_heads(col, src_rows, neg_rows, embeddings)
    pieces = [pieces[0]] + [shifted(pieces[s], s) for s in range(1, COLS)]

    weighted, factors = gather_tails(wanted, embeddings, relations)
    weighted = lax.all_to_all(
        weighted.reshape(OWNERS * COLS, PART, WIDTH), axes, split_axis=0, concat_axis=0, tiled=True
    ).reshape(OWNERS, COLS, PART, WIDTH)
    pulled, *grads = edge_scores(col, weighted, live, pieces)
    pulled = lax.all_to_all(
        pulled.reshape(OWNERS * COLS, PART, WIDTH), axes, split_axis=0, concat_axis=0, tiled=True
    ).reshape(SLOTS, WIDTH)
    grads = [grads[0]] + [shifted(grads[s], -s) for s in range(1, COLS)]
    gradient = scatter_heads(col, src_rows, neg_rows, grads)
    gradient = scatter_tails(wanted, gradient, factors, pulled)

    squares = jnp.sum(gradient * gradient, axis=1).reshape(-1, WIDTH)
    squares = (squares + shifted(squares, 2)) + (shifted(squares, 1) + shifted(squares, 3))
    new_state = adagrad_state + squares.reshape(-1) / (COLS * WIDTH)
    new_embeddings = embeddings - learning_rate * gradient / jnp.sqrt(new_state)[:, None]
    return (new_embeddings, new_state)


def solution(mesh):
    placed = (
        P("dom", "col"),
        P("dom"),
        P(None, "col"),
        P("dom"),
        P("dom"),
        P("dom"),
        P("dom", None),
        P("dom"),
    )
    return jax.shard_map(
        shards, mesh=mesh, in_specs=placed, out_specs=(P("dom", "col"), P("dom")), check_vma=False
    )
```

```python
import jax
import jax.numpy as jnp
from jax import lax
from jax.experimental import pallas as pl
from jax.experimental.pallas import tpu as pltpu
from jax.sharding import PartitionSpec as P

learning_rate = 0.3
OWNERS = 64
COLS = 4
PART = 16
BUCKET = COLS * PART
SLOTS = OWNERS * BUCKET
EDGES = OWNERS * PART
WIDTH = 128
FULL = COLS * WIDTH
NEG = 1000
NEG_PAD = 1024
HALF = 512
BLOCK = 256
CHAINS = 4

F32, BF16, I32 = jnp.float32, jnp.bfloat16, jnp.int32
SMEM = pl.BlockSpec(memory_space=pltpu.SMEM)
VMEM = pl.BlockSpec(memory_space=pltpu.VMEM)
HBM = pl.BlockSpec(memory_space=pltpu.HBM)
TABLE = pltpu.VMEM((SLOTS, WIDTH), F32)


def call(body, name, outs, ins, scratch, mib, flops=0, moved=0):
    return pl.pallas_call(
        body,
        out_shape=[shape for shape, _ in outs],
        in_specs=ins,
        out_specs=[spec for _, spec in outs],
        scratch_shapes=scratch,
        compiler_params=pltpu.CompilerParams(vmem_limit_bytes=mib * 1024 * 1024),
        cost_estimate=pl.CostEstimate(flops=flops, bytes_accessed=moved, transcendentals=0),
        name=name,
    )


def shape(rows, dtype, width=WIDTH):
    return jax.ShapeDtypeStruct((rows, width), dtype)


def rows_at(start, count):
    return pl.ds(start, count)


class Copies:
    def __init__(self, sems):
        self.sems, self.all = sems, []

    def start(self, source, target):
        self.all.append(pltpu.make_async_copy(source, target, self.sems.at[len(self.all)]))
        self.all[-1].start()

    def wait(self):
        for copy in self.all:
            copy.wait()


def gather_heads_body(col, src, neg, table, rounded, own, right, left, via_r, via_l, rows, corrupt, o, r, l, vr, vl, sems):
    copies = Copies(sems)
    rounded[...] = table[...].astype(BF16).astype(F32)

    @pl.loop(0, NEG // 40)
    def _(g):
        for i in range(40):
            corrupt[pl.ds(g * 40 + i, 1), :] = table[pl.ds(neg[g * 40 + i], 1), :]

    corrupt[NEG:NEG_PAD, :] = jnp.zeros((NEG_PAD - NEG, WIDTH), F32)
    first, second = corrupt[0:HALF, :].astype(BF16), corrupt[HALF:NEG_PAD, :].astype(BF16)

    @pl.loop(0, OWNERS)
    def _(b):
        for s in (2, 1, 3, 0):
            base = b * BUCKET + ((col[0] + s) & (COLS - 1)) * PART
            for i in range(PART):
                rows[pl.ds(s * EDGES + b * PART + i, 1), :] = table[pl.ds(src[base + i], 1), :]

    vr[0:HALF, :] = rows[2 * EDGES : 2 * EDGES + HALF, :].astype(BF16)
    vr[HALF:, :] = first
    copies.start(vr, via_r)
    vl[0:HALF, :] = rows[2 * EDGES + HALF : 3 * EDGES, :].astype(BF16)
    vl[HALF:, :] = second
    copies.start(vl, via_l)
    r[0:EDGES, :] = rows[EDGES : 2 * EDGES, :].astype(BF16)
    r[EDGES:, :] = second
    copies.start(r, right)
    l[0:EDGES, :] = rows[3 * EDGES :, :].astype(BF16)
    l[EDGES:, :] = first
    copies.start(l, left)
    o[0:EDGES, :] = rows[0:EDGES, :].astype(BF16)
    o[EDGES : EDGES + HALF, :] = first
    o[EDGES + HALF :, :] = second
    copies.start(o, own)
    copies.wait()


def gather_heads(col, src, neg, table):
    sizes = (EDGES + NEG_PAD, EDGES + HALF, EDGES + HALF, 2 * HALF, 2 * HALF)
    return call(
        gather_heads_body,
        "gather_heads",
        [(shape(SLOTS, F32), VMEM)] + [(shape(n, BF16), HBM) for n in sizes],
        [SMEM, SMEM, SMEM, VMEM],
        [TABLE, pltpu.VMEM((NEG_PAD, WIDTH), F32)]
        + [pltpu.VMEM((n, WIDTH), BF16) for n in sizes]
        + [pltpu.SemaphoreType.DMA((5,))],
        60,
        moved=20_000_000,
    )(col, src, neg, table)


def gather_tails_body(wanted, table, relations, out, rows, weighted, sems):
    copies = Copies(sems)
    for k in range(4):

        @pl.loop(k * OWNERS // 4, (k + 1) * OWNERS // 4)
        def _(b):
            for i in range(BUCKET):
                rows[pl.ds(b * BUCKET + i, 1), :] = (
                    table[pl.ds(wanted[b * 2 * BUCKET + i], 1), :]
                    * relations[pl.ds(wanted[b * 2 * BUCKET + BUCKET + i], 1), :]
                )

        part = pl.ds(k * SLOTS // 4, SLOTS // 4)
        weighted[part, :] = rows[part, :].astype(BF16)
        copies.start(weighted.at[part], out.at[part])
    copies.wait()


def gather_tails(wanted, table, relations):
    return call(
        gather_tails_body,
        "gather_tails",
        [(shape(SLOTS, BF16), HBM)],
        [SMEM, VMEM, VMEM],
        [TABLE, pltpu.VMEM((SLOTS, WIDTH), BF16), pltpu.SemaphoreType.DMA((4,))],
        60,
        flops=10_000_000_000,
        moved=20_000_000,
    )(wanted, table, relations)[0]


def gather_factors_body(wanted, relations, out):
    @pl.loop(0, OWNERS)
    def _(b):
        for i in range(BUCKET):
            row = wanted[b * 2 * BUCKET + BUCKET + i]
            out[pl.ds(b * BUCKET + i, 1), :] = relations[pl.ds(row, 1), :]


def gather_factors(wanted, relations):
    return call(
        gather_factors_body,
        "gather_factors",
        [(shape(SLOTS, F32), VMEM)],
        [SMEM, VMEM],
        [],
        60,
        moved=10_000_000,
    )(wanted, relations)[0]


def collect_body(own, dr, vr, dl, vl, wr, wl, heads, corrupt, *rest):
    held, sems = rest[:-1], rest[-1]
    copies = Copies(sems)
    for source, target in zip((own, dr, vr, dl, vl, wr, wl), held):
        copies.start(source, target)
    copies.wait()
    own, dr, vr, dl, vl, wr, wl = held
    span = [slice(s * WIDTH, (s + 1) * WIDTH) for s in range(COLS)]
    heads[:, span[0]] = own[0:EDGES, :]
    heads[:, span[1]] = dr[0:EDGES, :]
    heads[0:HALF, span[2]] = wr[0:HALF, :]
    heads[HALF:, span[2]] = wl[0:HALF, :]
    heads[:, span[3]] = dl[0:EDGES, :]
    corrupt[:, span[0]] = own[EDGES:, :]
    corrupt[0:HALF, span[1]] = vr[HALF:, :]
    corrupt[HALF:, span[1]] = dr[EDGES:, :]
    corrupt[0:HALF, span[2]] = wr[HALF:, :]
    corrupt[HALF:, span[2]] = wl[HALF:, :]
    corrupt[0:HALF, span[3]] = dl[EDGES:, :]
    corrupt[HALF:, span[3]] = vl[HALF:, :]


def collect(pieces):
    return call(
        collect_body,
        "collect",
        [(shape(EDGES, BF16, FULL), VMEM), (shape(NEG_PAD, BF16, FULL), VMEM)],
        [HBM] * 7,
        [pltpu.VMEM(p.shape, BF16) for p in pieces] + [pltpu.SemaphoreType.DMA((7,))],
        60,
        flops=19_000_000_000,
        moved=6_000_000,
    )(*pieces)


def edge_scores_body(col, counts, weighted, heads, corrupt, pulled_out, own, right, left, via_r, via_l, *rest):
    w, grad_scores, pulled, o, r, l, vr, vl, in_sems, out_sems = rest
    owner = [(col[0] + COLS - s) & (COLS - 1) for s in range(COLS)]
    span = [slice(s * WIDTH, (s + 1) * WIDTH) for s in range(COLS)]
    arrivals, copies = Copies(in_sems), Copies(out_sems)
    for s in range(COLS):
        arrivals.start(weighted.at[:, owner[s]], w.at[s])
    arrivals.wait()

    def send(values, at, second, where):
        n = values.shape[0]
        via, via_out = (vl, via_l) if second else (vr, via_r)
        for s, held, out, place in (
            (2, via, via_out, where),
            (1, l, left, at),
            (3, r, right, at),
            (0, o, own, at),
        ):
            held[place : place + n, :] = values[:, span[s]]
            copies.start(held.at[pl.ds(place, n)], out.at[pl.ds(place, n)])

    negatives = corrupt[...]
    slot = lax.broadcasted_iota(I32, (PART, 1), 0) + col[0] * PART
    buckets = BLOCK // PART
    whole = []
    for k in range(EDGES // BLOCK):
        rows = slice(k * BLOCK, (k + 1) * BLOCK)
        live = jnp.concatenate(
            [(slot < counts[0, b]).astype(F32) for b in range(k * buckets, (k + 1) * buckets)], axis=0
        )
        wk = jnp.concatenate(
            [w[s, k * buckets : (k + 1) * buckets].reshape(BLOCK, WIDTH) for s in range(COLS)], axis=1
        )
        whole.append(wk)
        wf, hf = wk.astype(F32), heads[rows, :].astype(F32)
        positive = jnp.sum(hf * wf, axis=1, keepdims=True)
        grad_positive = -live * jax.nn.sigmoid(-positive)
        scores = lax.dot_general(wk, negatives, (((1,), (1,)), ((), ())), preferred_element_type=F32)
        grad = (live * jax.nn.sigmoid(scores) * (1.0 / NEG)).astype(BF16)
        grad_scores[rows, :] = grad
        total = jnp.dot(grad, negatives, preferred_element_type=F32) + grad_positive * hf
        total = total.astype(BF16)
        place = pl.ds(k * buckets, buckets)
        for s in range(COLS):
            pulled[place, owner[s]] = total[:, span[s]].reshape(buckets, PART, WIDTH)
        copies.start(pulled.at[place], pulled_out.at[place])
        send((grad_positive * wf).astype(BF16), k * BLOCK, k * BLOCK >= HALF, k * BLOCK % HALF)
    weights = jnp.concatenate(whole, axis=0)
    for k in range(NEG_PAD // BLOCK):
        total = lax.dot_general(
            grad_scores[:, k * BLOCK : (k + 1) * BLOCK],
            weights,
            (((0,), (0,)), ((), ())),
            preferred_element_type=F32,
        )
        send(total.astype(BF16), EDGES + k * BLOCK, k * BLOCK >= HALF, HALF + k * BLOCK % HALF)
    copies.wait()


def edge_scores(col, counts, weighted, heads, corrupt):
    whole = (OWNERS, COLS, PART, WIDTH)
    sizes = (EDGES + NEG_PAD,) * 3 + (2 * HALF,) * 2
    return call(
        edge_scores_body,
        "edge_scores",
        [(jax.ShapeDtypeStruct(whole, BF16), HBM)] + [(shape(n, BF16), HBM) for n in sizes],
        [SMEM, SMEM, HBM, VMEM, VMEM],
        [
            pltpu.VMEM((COLS, OWNERS, PART, WIDTH), BF16),
            pltpu.VMEM((EDGES, NEG_PAD), BF16),
            pltpu.VMEM(whole, BF16),
        ]
        + [pltpu.VMEM((n, WIDTH), BF16) for n in sizes]
        + [pltpu.SemaphoreType.DMA((COLS,)), pltpu.SemaphoreType.DMA((36,))],
        60,
        flops=3_200_000_000,
        moved=8_000_000,
    )(col, counts, weighted, heads, corrupt)


def begin(tables, start=None):
    for n, table in enumerate(tables):
        if n > 0 or start is None:
            table[...] = jnp.zeros((SLOTS, WIDTH), F32)
        else:
            table[...] = start[...]


def finish(tables):
    total = tables[0][...]
    for table in tables[1:]:
        total += table[...]
    tables[0][...] = total


def scatter_near_body(col, src, g0, g1, g3, out, b0, b1, b3, r0, r1, r3, sems, *tables):
    tables = (out,) + tables
    copies = Copies(sems)
    for source, target in ((g0, b0), (g1, b1), (g3, b3)):
        copies.start(source.at[pl.ds(0, EDGES)], target)
    begin(tables)
    copies.wait()
    for source, target in ((b0, r0), (b1, r1), (b3, r3)):
        target[...] = source[...].astype(F32)

    @pl.loop(0, OWNERS)
    def _(b):
        for i in range(PART):
            for s, rows in ((0, r0), (1, r1), (3, r3)):
                base = b * BUCKET + ((col[0] + s) & (COLS - 1)) * PART
                into = tables[(i * 3 + s) % CHAINS]
                into[pl.ds(src[base + i], 1), :] += rows[pl.ds(b * PART + i, 1), :]

    finish(tables)


def scatter_near(col, src, g0, g1, g3):
    return call(
        scatter_near_body,
        "scatter_near",
        [(shape(SLOTS, F32), VMEM)],
        [SMEM] * 2 + [HBM] * 3,
        [pltpu.VMEM((EDGES, WIDTH), BF16)] * 3
        + [pltpu.VMEM((EDGES, WIDTH), F32)] * 3
        + [pltpu.SemaphoreType.DMA((3,))]
        + [TABLE] * (CHAINS - 1),
        60,
        flops=10_000_000_000,
        moved=20_000_000,
    )(col, src, g0, g1, g3)[0]


def scatter_far_body(col, src, neg, start, g0, g1, g3, wr, wl, out, b0, b1, b3, br, bl, rr, rl, corrupt, sems, *tables):
    tables = (out,) + tables
    copies = Copies(sems)
    copies.start(wr, br)
    copies.start(wl, bl)
    for source, target in ((g0, b0), (g1, b1), (g3, b3)):
        copies.start(source.at[pl.ds(EDGES, NEG_PAD)], target)
    begin(tables, start)
    copies.wait()
    rr[...] = br[0:HALF, :].astype(F32)
    rl[...] = bl[0:HALF, :].astype(F32)
    near = b0[...].astype(F32) + b1[...].astype(F32) + b3[...].astype(F32)
    corrupt[0:HALF, :] = near[0:HALF, :] + br[HALF:, :].astype(F32)
    corrupt[HALF:, :] = near[HALF:, :] + bl[HALF:, :].astype(F32)

    @pl.loop(0, OWNERS // 2)
    def _(b):
        for i in range(PART):
            for n, rows in enumerate((rr, rl)):
                base = (b + n * OWNERS // 2) * BUCKET + ((col[0] + 2) & (COLS - 1)) * PART
                into = tables[(i * 2 + n) % CHAINS]
                into[pl.ds(src[base + i], 1), :] += rows[pl.ds(b * PART + i, 1), :]

    @pl.loop(0, NEG // 40)
    def _(g):
        for i in range(40):
            into = tables[i % CHAINS]
            into[pl.ds(neg[g * 40 + i], 1), :] += corrupt[pl.ds(g * 40 + i, 1), :]

    finish(tables)


def scatter_far(col, src, neg, start, g0, g1, g3, wr, wl):
    return call(
        scatter_far_body,
        "scatter_far",
        [(shape(SLOTS, F32), VMEM)],
        [SMEM] * 3 + [VMEM] + [HBM] * 5,
        [pltpu.VMEM((NEG_PAD, WIDTH), BF16)] * 5
        + [pltpu.VMEM((HALF, WIDTH), F32)] * 2
        + [pltpu.VMEM((NEG_PAD, WIDTH), F32), pltpu.SemaphoreType.DMA((5,))]
        + [TABLE] * (CHAINS - 1),
        60,
        flops=10_000_000_000,
        moved=20_000_000,
    )(col, src, neg, start, g0, g1, g3, wr, wl)[0]


def scatter_tails_body(wanted, start, factors, pulled, out, held, rows, sems, *tables):
    tables = (out,) + tables
    copies = Copies(sems)
    copies.start(pulled, held)
    begin(tables, start)
    copies.wait()
    rows[...] = factors[...] * held[...].astype(F32)

    @pl.loop(0, OWNERS)
    def _(b):
        for i in range(BUCKET):
            into = tables[i % CHAINS]
            into[pl.ds(wanted[b * 2 * BUCKET + i], 1), :] += rows[pl.ds(b * BUCKET + i, 1), :]

    finish(tables)


def scatter_tails(wanted, start, factors, pulled):
    return call(
        scatter_tails_body,
        "scatter_tails",
        [(shape(SLOTS, F32), VMEM)],
        [SMEM] + [VMEM] * 2 + [HBM],
        [pltpu.VMEM((SLOTS, WIDTH), BF16), TABLE, pltpu.SemaphoreType.DMA((1,))] + [TABLE] * (CHAINS - 1),
        60,
        moved=30_000_000,
    )(wanted, start, factors, pulled)[0]


def shifted(x, s):
    return lax.ppermute(x, "col", [(i, (i + s) % COLS) for i in range(COLS)])


def exchanged(right, left, via_r, via_l):
    vr, vl = shifted(via_r, 1), shifted(via_l, -1)
    dr, dl = shifted(right, 1), shifted(left, -1)
    return dr, vr, dl, vl, shifted(vr, 1), shifted(vl, -1)


def shards(
    embeddings, adagrad_state, relations, src_rows, dst_rows, rel_ids, bucket_counts, neg_rows
):
    axes = ("dom", "col")
    col = lax.axis_index("col").astype(I32).reshape(1)

    def sent(x):
        return lax.all_to_all(
            x.reshape(OWNERS * COLS, PART, WIDTH), axes, split_axis=0, concat_axis=0, tiled=True
        )

    words = jnp.concatenate([dst_rows.reshape(OWNERS, BUCKET), rel_ids.reshape(OWNERS, BUCKET)], axis=1)
    wanted = lax.all_to_all(words, "dom", split_axis=0, concat_axis=0, tiled=True).reshape(2 * SLOTS)
    rounded, own, *outgoing = gather_heads(col, src_rows, neg_rows, embeddings)
    weighted = sent(gather_tails(wanted, rounded, relations))
    heads, corrupt = collect([own, *exchanged(*outgoing)])
    pulled, own, *outgoing = edge_scores(
        col, bucket_counts, weighted.reshape(OWNERS, COLS, PART, WIDTH), heads, corrupt
    )
    pulled = sent(pulled).reshape(SLOTS, WIDTH)
    from_left, _, from_right, _, far_a, far_b = exchanged(*outgoing)
    gradient = scatter_near(col, src_rows, own, from_right, from_left)
    gradient = scatter_far(col, src_rows, neg_rows, gradient, own, from_right, from_left, far_a, far_b)
    gradient = scatter_tails(wanted, gradient, gather_factors(wanted, relations), pulled)

    squares = jnp.sum(gradient * gradient, axis=1).reshape(-1, WIDTH)
    squares = (squares + shifted(squares, 2)) + (shifted(squares, 1) + shifted(squares, 3))
    new_state = adagrad_state + squares.reshape(-1) / FULL
    new_embeddings = embeddings - learning_rate * gradient / jnp.sqrt(new_state)[:, None]
    return (new_embeddings, new_state)


def solution(mesh):
    placed = (
        P("dom", "col"),
        P("dom"),
        P(None, "col"),
        P("dom"),
        P("dom"),
        P("dom"),
        P("dom", None),
        P("dom"),
    )
    return jax.shard_map(
        shards, mesh=mesh, in_specs=placed, out_specs=(P("dom", "col"), P("dom")), check_vma=False
    )
```

```python
import jax
import jax.numpy as jnp
from jax import lax
from jax.experimental import pallas as pl
from jax.experimental.pallas import tpu as pltpu
from jax.sharding import PartitionSpec as P

learning_rate = 0.3
OWNERS = 64
COLS = 4
PART = 16
BUCKET = COLS * PART
SLOTS = OWNERS * BUCKET
EDGES = OWNERS * PART
WIDTH = 128
FULL = COLS * WIDTH
NEG = 1000
NEG_PAD = 1024
DIRECT = EDGES + NEG_PAD
HALF = 512
BLOCK = 256
CHAINS = 4
WHOLE = 65_300

F32, BF16, I32 = jnp.float32, jnp.bfloat16, jnp.int32
SMEM = pl.BlockSpec(memory_space=pltpu.SMEM)
VMEM = pl.BlockSpec(memory_space=pltpu.VMEM)
HBM = pl.BlockSpec(memory_space=pltpu.HBM)
TABLE = pltpu.VMEM((SLOTS, WIDTH), F32)


def call(body, name, outs, ins, scratch, kib=WHOLE, flops=0, moved=0):
    return pl.pallas_call(
        body,
        out_shape=[shape for shape, _ in outs],
        in_specs=ins,
        out_specs=[spec for _, spec in outs],
        scratch_shapes=scratch,
        compiler_params=pltpu.CompilerParams(vmem_limit_bytes=kib * 1024),
        cost_estimate=pl.CostEstimate(flops=flops, bytes_accessed=moved, transcendentals=0),
        name=name,
    )


def shape(rows, dtype, width=WIDTH):
    return jax.ShapeDtypeStruct((rows, width), dtype)


def rows_at(start, count):
    return pl.ds(start, count)


class Copies:
    def __init__(self, sems):
        self.sems, self.all = sems, []

    def start(self, source, target):
        self.all.append(pltpu.make_async_copy(source, target, self.sems.at[len(self.all)]))
        self.all[-1].start()

    def wait(self):
        for copy in self.all:
            copy.wait()


def head_rows(place, src, table, rows, pieces):
    @pl.loop(0, OWNERS)
    def _(b):
        for n, s in enumerate(pieces):
            base = b * BUCKET + ((place[0] + s) & (COLS - 1)) * PART
            for i in range(PART):
                rows[pl.ds(n * EDGES + b * PART + i, 1), :] = table[pl.ds(src[base + i], 1), :]


def gather_far_body(place, src, neg, table, via_r, via_l, corrupt_out, rows, corrupt, rounded, vr, vl, sems):
    copies = Copies(sems)

    @pl.loop(0, NEG // 40)
    def _(g):
        for i in range(40):
            corrupt[pl.ds(g * 40 + i, 1), :] = table[pl.ds(neg[g * 40 + i], 1), :]

    corrupt[NEG:NEG_PAD, :] = jnp.zeros((NEG_PAD - NEG, WIDTH), F32)
    rounded[...] = corrupt[...].astype(BF16)
    copies.start(rounded, corrupt_out)
    head_rows(place, src, table, rows, (2,))
    for held, out, part in ((vr, via_r, slice(0, HALF)), (vl, via_l, slice(HALF, 2 * HALF))):
        held[0:HALF, :] = rows[part, :].astype(BF16)
        held[HALF:, :] = rounded[part, :]
        copies.start(held, out)
    copies.wait()


def gather_far(place, src, neg, table):
    return call(
        gather_far_body,
        "gather_far",
        [(shape(2 * HALF, BF16), HBM)] * 3,
        [SMEM, SMEM, SMEM, VMEM],
        [pltpu.VMEM((EDGES, WIDTH), F32), pltpu.VMEM((NEG_PAD, WIDTH), F32)]
        + [pltpu.VMEM((2 * HALF, WIDTH), BF16)] * 3
        + [pltpu.SemaphoreType.DMA((3,))],
        WHOLE,
        moved=10_000_000,
    )(place, src, neg, table)


def gather_near_body(place, src, table, corrupt, right, left, rows, halves, r, l, in_sems, sems):
    arrivals, copies = Copies(in_sems), Copies(sems)
    arrivals.start(corrupt, halves)
    head_rows(place, src, table, rows, (1, 3))
    arrivals.wait()
    r[0:EDGES, :] = rows[0:EDGES, :].astype(BF16)
    r[EDGES:, :] = halves[HALF:, :]
    copies.start(r, right)
    l[0:EDGES, :] = rows[EDGES : 2 * EDGES, :].astype(BF16)
    l[EDGES:, :] = halves[0:HALF, :]
    copies.start(l, left)
    copies.wait()


def gather_near(place, src, table, corrupt):
    sizes = (EDGES + HALF, EDGES + HALF)
    return call(
        gather_near_body,
        "gather_near",
        [(shape(n, BF16), HBM) for n in sizes],
        [SMEM, SMEM, VMEM, HBM],
        [pltpu.VMEM((2 * EDGES, WIDTH), F32), pltpu.VMEM((NEG_PAD, WIDTH), BF16)]
        + [pltpu.VMEM((n, WIDTH), BF16) for n in sizes]
        + [pltpu.SemaphoreType.DMA((1,)), pltpu.SemaphoreType.DMA((2,))],
        WHOLE,
        flops=17_000_000_000,
        moved=20_000_000,
    )(place, src, table, corrupt)


LINES = 4 * BUCKET


def gather_tails_body(place, wanted, table, relations, out, factors_out, words, rows, factors, weighted, sems):
    copies = Copies(sems)
    copies.start(wanted, words)
    for k in range(4):

        @pl.loop(k * OWNERS // 4, (k + 1) * OWNERS // 4)
        def _(b):
            base = b * LINES + place[1] * BUCKET
            for i in range(BUCKET):
                rows[pl.ds(b * BUCKET + i, 1), :] = table[pl.ds(wanted[base + i], 1), :]
                row = wanted[base + 2 * BUCKET + i]
                factors[pl.ds(b * BUCKET + i, 1), :] = relations[pl.ds(row, 1), :]

        part = pl.ds(k * SLOTS // 4, SLOTS // 4)
        weighted[part, :] = (factors[part, :] * rows[part, :].astype(BF16).astype(F32)).astype(BF16)
        copies.start(weighted.at[part], out.at[part])
        copies.start(factors.at[part], factors_out.at[part])
    copies.wait()


def gather_tails(place, wanted, table, relations):
    return call(
        gather_tails_body,
        "gather_tails",
        [
            (shape(SLOTS, BF16), HBM),
            (shape(SLOTS, F32), HBM),
            (jax.ShapeDtypeStruct((OWNERS * LINES,), I32), HBM),
        ],
        [SMEM, SMEM, VMEM, VMEM],
        [TABLE, TABLE, pltpu.VMEM((SLOTS, WIDTH), BF16), pltpu.SemaphoreType.DMA((9,))],
        WHOLE,
        flops=10_000_000_000,
        moved=20_000_000,
    )(place, wanted, table, relations)


def gather_own_body(place, src, table, out, rows, held, sems):
    copies = Copies(sems)
    head_rows(place, src, table, rows, (0,))
    held[...] = rows[...].astype(BF16)
    copies.start(held, out)
    copies.wait()


def gather_own(place, src, table):
    return call(
        gather_own_body,
        "gather_own",
        [(shape(EDGES, BF16), HBM)],
        [SMEM, SMEM, VMEM],
        [
            pltpu.VMEM((EDGES, WIDTH), F32),
            pltpu.VMEM((EDGES, WIDTH), BF16),
            pltpu.SemaphoreType.DMA((1,)),
        ],
        WHOLE,
        moved=3_000_000,
    )(place, src, table)[0]


def edge_scores_body(
    place, counts, weighted_in, h0, n0, dr, vr, dl, vl, wr, wl, pulled_out, own, right, left, *rest
):
    weighted, heads, corrupt, grad_scores, pulled, o, r, l, in_sems, sems = rest
    owner = [(place[0] + COLS - s) & (COLS - 1) for s in range(COLS)]
    span = [slice(s * WIDTH, (s + 1) * WIDTH) for s in range(COLS)]
    arrivals, copies = Copies(in_sems), Copies(sems)

    def fetch(source, begin, target, row, s, n):
        arrivals.start(source.at[pl.ds(begin, n)], target.at[pl.ds(row, n), pl.ds(s * WIDTH, WIDTH)])

    fetch(n0, 0, corrupt, 0, 0, NEG_PAD)
    fetch(vr, HALF, corrupt, 0, 1, HALF)
    fetch(dr, EDGES, corrupt, HALF, 1, HALF)
    fetch(wr, HALF, corrupt, 0, 2, HALF)
    fetch(wl, HALF, corrupt, HALF, 2, HALF)
    fetch(dl, EDGES, corrupt, 0, 3, HALF)
    fetch(vl, HALF, corrupt, HALF, 3, HALF)
    arrivals.start(weighted_in, weighted)
    fetch(h0, 0, heads, 0, 0, EDGES)
    fetch(dr, 0, heads, 0, 1, EDGES)
    fetch(wr, 0, heads, 0, 2, HALF)
    fetch(wl, 0, heads, HALF, 2, HALF)
    fetch(dl, 0, heads, 0, 3, EDGES)
    arrivals.wait()

    def send(values, at, where, second):
        n = values.shape[0]
        via, via_out = (l, left) if second else (r, right)
        for s, held, out, begins in ((2, via, via_out, where), (1, l, left, at), (3, r, right, at), (0, o, own, at)):
            held[begins : begins + n, :] = values[:, span[s]]
            copies.start(held.at[pl.ds(begins, n)], out.at[pl.ds(begins, n)])

    negatives = corrupt[...]
    slot = lax.broadcasted_iota(I32, (PART, 1), 0) + place[0] * PART
    buckets = BLOCK // PART
    whole = []
    for k in range(EDGES // BLOCK):
        rows = slice(k * BLOCK, (k + 1) * BLOCK)
        live = jnp.concatenate(
            [(slot < counts[0, b]).astype(F32) for b in range(k * buckets, (k + 1) * buckets)], axis=0
        )
        wk = jnp.concatenate(
            [weighted[k * buckets : (k + 1) * buckets, owner[s]].reshape(BLOCK, WIDTH) for s in range(COLS)],
            axis=1,
        )
        whole.append(wk)
        wf, hf = wk.astype(F32), heads[rows, :].astype(F32)
        positive = jnp.sum(hf * wf, axis=1, keepdims=True)
        grad_positive = -live * jax.nn.sigmoid(-positive)
        scores = lax.dot_general(wk, negatives, (((1,), (1,)), ((), ())), preferred_element_type=F32)
        grad = (live * jax.nn.sigmoid(scores) * (1.0 / NEG)).astype(BF16)
        grad_scores[rows, :] = grad
        total = jnp.dot(grad, negatives, preferred_element_type=F32) + grad_positive * hf
        total = total.astype(BF16)
        at = pl.ds(k * buckets, buckets)
        for s in range(COLS):
            pulled[at, owner[s]] = total[:, span[s]].reshape(buckets, PART, WIDTH)
        copies.start(pulled.at[at], pulled_out.at[at])
        send((grad_positive * wf).astype(BF16), k * BLOCK, DIRECT + k * BLOCK % HALF, k * BLOCK >= HALF)
    weights = jnp.concatenate(whole, axis=0)
    for k in range(NEG_PAD // BLOCK):
        total = lax.dot_general(
            grad_scores[:, k * BLOCK : (k + 1) * BLOCK],
            weights,
            (((0,), (0,)), ((), ())),
            preferred_element_type=F32,
        )
        send(
            total.astype(BF16),
            EDGES + k * BLOCK,
            DIRECT + HALF + k * BLOCK % HALF,
            k * BLOCK >= HALF,
        )
    copies.wait()


def edge_scores(place, counts, weighted, pieces):
    whole = (OWNERS, COLS, PART, WIDTH)
    sizes = (DIRECT, DIRECT + 2 * HALF, DIRECT + 2 * HALF)
    return call(
        edge_scores_body,
        "edge_scores",
        [(jax.ShapeDtypeStruct(whole, BF16), HBM)] + [(shape(n, BF16), HBM) for n in sizes],
        [SMEM, SMEM] + [HBM] * 9,
        [
            pltpu.VMEM(whole, BF16),
            pltpu.VMEM((EDGES, FULL), BF16),
            pltpu.VMEM((NEG_PAD, FULL), BF16),
            pltpu.VMEM((EDGES, NEG_PAD), BF16),
            pltpu.VMEM(whole, BF16),
        ]
        + [pltpu.VMEM((n, WIDTH), BF16) for n in sizes]
        + [pltpu.SemaphoreType.DMA((13,)), pltpu.SemaphoreType.DMA((36,))],
        WHOLE,
        flops=3_200_000_000,
        moved=8_000_000,
    )(place, counts, weighted, *pieces)


def begin(tables, start=None):
    for n, table in enumerate(tables):
        if n > 0 or start is None:
            table[...] = jnp.zeros((SLOTS, WIDTH), F32)
        else:
            table[...] = start[...]


def finish(tables):
    total = tables[0][...]
    for table in tables[1:]:
        total += table[...]
    tables[0][...] = total


def scatter_near_body(col, src, g0, g1, g3, out, b0, b1, b3, r0, r1, r3, sems, *tables):
    tables = (out,) + tables
    copies = Copies(sems)
    for source, target in ((g0, b0), (g1, b1), (g3, b3)):
        copies.start(source.at[pl.ds(0, EDGES)], target)
    begin(tables)
    copies.wait()
    for source, target in ((b0, r0), (b1, r1), (b3, r3)):
        target[...] = source[...].astype(F32)

    @pl.loop(0, OWNERS)
    def _(b):
        for i in range(PART):
            for s, rows in ((0, r0), (1, r1), (3, r3)):
                base = b * BUCKET + ((col[0] + s) & (COLS - 1)) * PART
                into = tables[(i * 3 + s) % CHAINS]
                into[pl.ds(src[base + i], 1), :] += rows[pl.ds(b * PART + i, 1), :]

    finish(tables)


def scatter_near(col, src, g0, g1, g3):
    return call(
        scatter_near_body,
        "scatter_near",
        [(shape(SLOTS, F32), VMEM)],
        [SMEM] * 2 + [HBM] * 3,
        [pltpu.VMEM((EDGES, WIDTH), BF16)] * 3
        + [pltpu.VMEM((EDGES, WIDTH), F32)] * 3
        + [pltpu.SemaphoreType.DMA((3,))]
        + [TABLE] * (CHAINS - 1),
        WHOLE,
        flops=10_000_000_000,
        moved=20_000_000,
    )(col, src, g0, g1, g3)[0]


def scatter_far_body(col, src, neg, start, g0, g1, g3, wr, wl, out, b0, b1, b3, br, bl, rr, rl, corrupt, sems, *tables):
    tables = (out,) + tables
    copies = Copies(sems)
    copies.start(wr, br)
    copies.start(wl, bl)
    for source, target in ((g0, b0), (g1, b1), (g3, b3)):
        copies.start(source.at[pl.ds(EDGES, NEG_PAD)], target)
    begin(tables, start)
    copies.wait()
    rr[...] = br[0:HALF, :].astype(F32)
    rl[...] = bl[0:HALF, :].astype(F32)
    near = b0[...].astype(F32) + b1[...].astype(F32) + b3[...].astype(F32)
    corrupt[0:HALF, :] = near[0:HALF, :] + br[HALF:, :].astype(F32)
    corrupt[HALF:, :] = near[HALF:, :] + bl[HALF:, :].astype(F32)

    @pl.loop(0, OWNERS // 2)
    def _(b):
        for i in range(PART):
            for n, rows in enumerate((rr, rl)):
                base = (b + n * OWNERS // 2) * BUCKET + ((col[0] + 2) & (COLS - 1)) * PART
                into = tables[(i * 2 + n) % CHAINS]
                into[pl.ds(src[base + i], 1), :] += rows[pl.ds(b * PART + i, 1), :]

    @pl.loop(0, NEG // 40)
    def _(g):
        for i in range(40):
            into = tables[i % CHAINS]
            into[pl.ds(neg[g * 40 + i], 1), :] += corrupt[pl.ds(g * 40 + i, 1), :]

    finish(tables)


def scatter_far(col, src, neg, start, g0, g1, g3, wr, wl):
    return call(
        scatter_far_body,
        "scatter_far",
        [(shape(SLOTS, F32), VMEM)],
        [SMEM] * 3 + [VMEM] + [HBM] * 5,
        [pltpu.VMEM((NEG_PAD, WIDTH), BF16)] * 5
        + [pltpu.VMEM((HALF, WIDTH), F32)] * 2
        + [pltpu.VMEM((NEG_PAD, WIDTH), F32), pltpu.SemaphoreType.DMA((5,))]
        + [TABLE] * (CHAINS - 1),
        WHOLE,
        flops=10_000_000_000,
        moved=20_000_000,
    )(col, src, neg, start, g0, g1, g3, wr, wl)[0]


def scatter_tails_body(place, wanted, start, factors, pulled, out, squares, held, scale, rows, first, in_sems, *tables):
    arrivals = []
    parts = [pl.ds(k * SLOTS // 4, SLOTS // 4) for k in range(4)]
    for k, part in enumerate(parts):
        for n, (source, target) in enumerate(((pulled, held), (factors, scale))):
            arrivals.append(pltpu.make_async_copy(source.at[part], target.at[part], in_sems.at[2 * k + n]))
            arrivals[-1].start()
    arrivals.append(pltpu.make_async_copy(start, first, in_sems.at[8]))
    arrivals[-1].start()
    begin(tables)
    for k, part in enumerate(parts):
        arrivals[2 * k].wait()
        arrivals[2 * k + 1].wait()
        rows[part, :] = scale[part, :] * held[part, :].astype(F32)

        @pl.loop(k * OWNERS // 4, (k + 1) * OWNERS // 4)
        def _(b):
            base = b * LINES + place[1] * BUCKET
            for i in range(BUCKET):
                into = tables[i % CHAINS]
                into[pl.ds(wanted[base + i], 1), :] += rows[pl.ds(b * BUCKET + i, 1), :]

    arrivals[-1].wait()
    ones = jnp.ones((16, 2 * WIDTH), BF16)
    for k, part in enumerate(parts):
        total = first[part, :]
        for table in tables:
            total += table[part, :]
        out[part, :] = total
        square = total * total
        high = square.astype(BF16)
        low = (square - high.astype(F32)).astype(BF16)
        sums = lax.dot_general(
            ones, jnp.concatenate([high, low], axis=1), (((1,), (1,)), ((), ())), preferred_element_type=F32
        )
        for n in range(SLOTS // 4 // WIDTH):
            line = k * SLOTS // 4 // WIDTH + n
            squares[line : line + 1, :] = sums[0:1, n * WIDTH : (n + 1) * WIDTH]


def scatter_tails(place, wanted, start, factors, pulled):
    return call(
        scatter_tails_body,
        "scatter_tails",
        [(shape(SLOTS, F32), VMEM), (shape(SLOTS // WIDTH, F32), VMEM)],
        [SMEM] * 2 + [HBM] * 3,
        [pltpu.VMEM((SLOTS, WIDTH), BF16), TABLE, TABLE, TABLE]
        + [pltpu.SemaphoreType.DMA((9,))]
        + [TABLE] * CHAINS,
        WHOLE,
        moved=30_000_000,
    )(place, wanted, start, factors, pulled)


def stage_body(table, gradient, table_out, step_out):
    table_out[...] = table[...]
    step_out[...] = gradient[...] * learning_rate


def stage(table, gradient):
    return call(
        stage_body,
        "stage",
        [(shape(SLOTS, F32), VMEM)] * 2,
        [VMEM] * 2,
        [],
        12 * 1024,
        moved=8_000_000,
    )(table, gradient)


def shifted(x, s):
    return lax.ppermute(x, "col", [(i, (i + s) % COLS) for i in range(COLS)])


def shards(
    embeddings, adagrad_state, relations, src_rows, dst_rows, rel_ids, bucket_counts, neg_rows
):
    axes = ("dom", "col")
    place = jnp.stack([lax.axis_index("col"), lax.axis_index("dom") & 1]).astype(I32)

    def sent(x):
        return lax.all_to_all(
            x.reshape(OWNERS * COLS, PART, WIDTH), axes, split_axis=0, concat_axis=0, tiled=True
        )

    pairs = (OWNERS // 2, 2, 2, WIDTH)
    rows, kinds = (lax.broadcast_in_dim(x.reshape(-1, WIDTH), pairs, (0, 3)) for x in (dst_rows, rel_ids))
    words = jnp.where(lax.broadcasted_iota(I32, pairs, 2) == 0, rows, kinds).reshape(OWNERS, 2, WIDTH)
    wanted = lax.all_to_all(words, "dom", split_axis=0, concat_axis=0, tiled=True).reshape(-1)

    via_r, via_l, negatives = gather_far(place, src_rows, neg_rows, embeddings)
    vr, vl = shifted(via_r, 1), shifted(via_l, -1)
    weighted, factors, wanted = gather_tails(place, wanted, embeddings, relations)
    weighted = sent(weighted).reshape(OWNERS, COLS, PART, WIDTH)
    after, factors, vr, vl = lax.optimization_barrier((negatives, factors, vr, vl))
    right, left = gather_near(place, src_rows, embeddings, after)
    heads = gather_own(place, src_rows, embeddings)
    pieces = [heads, after, shifted(right, 1), vr, shifted(left, -1), vl, shifted(vr, 1), shifted(vl, -1)]
    pulled, own, right, left = edge_scores(place, bucket_counts, weighted, pieces)
    pulled = sent(pulled).reshape(SLOTS, WIDTH)
    from_left, from_right = shifted(right, 1), shifted(left, -1)
    far_a, far_b = shifted(from_left[DIRECT:], 1), shifted(from_right[DIRECT:], -1)
    gradient = scatter_near(place, src_rows, own, from_right, from_left)
    gradient = scatter_far(place, src_rows, neg_rows, gradient, own, from_right, from_left, far_a, far_b)
    gradient, squares = scatter_tails(place, wanted, gradient, factors, pulled)

    table, step = stage(embeddings, gradient)
    squares = (squares + shifted(squares, 2)) + (shifted(squares, 1) + shifted(squares, 3))
    new_state = adagrad_state + squares.reshape(-1) / FULL
    new_embeddings = table - step / jnp.sqrt(new_state)[:, None]
    return (new_embeddings, new_state)


def solution(mesh):
    placed = (
        P("dom", "col"),
        P("dom"),
        P(None, "col"),
        P("dom"),
        P("dom"),
        P("dom"),
        P("dom", None),
        P("dom"),
    )
    return jax.shard_map(
        shards, mesh=mesh, in_specs=placed, out_specs=(P("dom", "col"), P("dom")), check_vma=False
    )
```

```python
import jax
import jax.numpy as jnp
from jax import lax
from jax.experimental import pallas as pl
from jax.experimental.pallas import tpu as pltpu
from jax.sharding import PartitionSpec as P

learning_rate = 0.3
OWNERS = 64
COLS = 4
PART = 16
BUCKET = COLS * PART
SLOTS = OWNERS * BUCKET
EDGES = OWNERS * PART
WIDTH = 128
FULL = COLS * WIDTH
NEG = 1000
NEG_PAD = 1024
DIRECT = EDGES + NEG_PAD
HALF = 512
BLOCK = 256
CHAINS = 8
WHOLE = 65_300

F32, BF16, I32 = jnp.float32, jnp.bfloat16, jnp.int32
SMEM = pl.BlockSpec(memory_space=pltpu.SMEM)
VMEM = pl.BlockSpec(memory_space=pltpu.VMEM)
HBM = pl.BlockSpec(memory_space=pltpu.HBM)
TABLE = pltpu.VMEM((SLOTS, WIDTH), F32)


def call(body, name, outs, ins, scratch, kib=WHOLE, flops=0, moved=0):
    return pl.pallas_call(
        body,
        out_shape=[shape for shape, _ in outs],
        in_specs=ins,
        out_specs=[spec for _, spec in outs],
        scratch_shapes=scratch,
        compiler_params=pltpu.CompilerParams(vmem_limit_bytes=kib * 1024),
        cost_estimate=pl.CostEstimate(flops=flops, bytes_accessed=moved, transcendentals=0),
        name=name,
    )


def shape(rows, dtype, width=WIDTH):
    return jax.ShapeDtypeStruct((rows, width), dtype)


def rows_at(start, count):
    return pl.ds(start, count)


class Copies:
    def __init__(self, sems):
        self.sems, self.all = sems, []

    def start(self, source, target):
        self.all.append(pltpu.make_async_copy(source, target, self.sems.at[len(self.all)]))
        self.all[-1].start()
        return self.all[-1]

    def wait(self):
        for copy in self.all:
            copy.wait()


def head_rows(place, src, table, rows, pieces):
    @pl.loop(0, OWNERS)
    def _(b):
        for n, s in enumerate(pieces):
            base = b * BUCKET + ((place[0] + s) & (COLS - 1)) * PART
            for i in range(PART):
                rows[pl.ds(n * EDGES + b * PART + i, 1), :] = table[pl.ds(src[base + i], 1), :]


def gather_far_body(place, src, neg, table, via_r, via_l, corrupt_out, rows, corrupt, rounded, vr, vl, sems):
    copies = Copies(sems)

    @pl.loop(0, NEG // 40)
    def _(g):
        for i in range(40):
            corrupt[pl.ds(g * 40 + i, 1), :] = table[pl.ds(neg[g * 40 + i], 1), :]

    corrupt[NEG:NEG_PAD, :] = jnp.zeros((NEG_PAD - NEG, WIDTH), F32)
    rounded[...] = corrupt[...].astype(BF16)
    copies.start(rounded, corrupt_out)
    head_rows(place, src, table, rows, (2,))
    for held, out, part in ((vr, via_r, slice(0, HALF)), (vl, via_l, slice(HALF, 2 * HALF))):
        held[0:HALF, :] = rows[part, :].astype(BF16)
        held[HALF:, :] = rounded[part, :]
        copies.start(held, out)
    copies.wait()


def gather_far(place, src, neg, table):
    return call(
        gather_far_body,
        "gather_far",
        [(shape(2 * HALF, BF16), HBM)] * 3,
        [SMEM, SMEM, SMEM, VMEM],
        [pltpu.VMEM((EDGES, WIDTH), F32), pltpu.VMEM((NEG_PAD, WIDTH), F32)]
        + [pltpu.VMEM((2 * HALF, WIDTH), BF16)] * 3
        + [pltpu.SemaphoreType.DMA((3,))],
        WHOLE,
        moved=10_000_000,
    )(place, src, neg, table)


def gather_near_body(place, src, table, corrupt, right, left, rows, halves, r, l, in_sems, sems):
    arrivals, copies = Copies(in_sems), Copies(sems)
    arrivals.start(corrupt, halves)
    head_rows(place, src, table, rows, (1, 3))
    arrivals.wait()
    r[0:EDGES, :] = rows[0:EDGES, :].astype(BF16)
    r[EDGES:, :] = halves[HALF:, :]
    copies.start(r, right)
    l[0:EDGES, :] = rows[EDGES : 2 * EDGES, :].astype(BF16)
    l[EDGES:, :] = halves[0:HALF, :]
    copies.start(l, left)
    copies.wait()


def gather_near(place, src, table, corrupt):
    sizes = (EDGES + HALF, EDGES + HALF)
    return call(
        gather_near_body,
        "gather_near",
        [(shape(n, BF16), HBM) for n in sizes],
        [SMEM, SMEM, VMEM, HBM],
        [pltpu.VMEM((2 * EDGES, WIDTH), F32), pltpu.VMEM((NEG_PAD, WIDTH), BF16)]
        + [pltpu.VMEM((n, WIDTH), BF16) for n in sizes]
        + [pltpu.SemaphoreType.DMA((1,)), pltpu.SemaphoreType.DMA((2,))],
        WHOLE,
        flops=17_000_000_000,
        moved=20_000_000,
    )(place, src, table, corrupt)


LINE = 2 * BUCKET


def request_body(rows, kinds, out):
    first = lax.broadcasted_iota(I32, (OWNERS // 2, WIDTH), 1) < BUCKET
    rows, kinds = rows[...], kinds[...]
    out[pl.ds(0, OWNERS // 2, stride=2), :] = jnp.where(first, rows, pltpu.roll(kinds, BUCKET, 1))
    out[pl.ds(1, OWNERS // 2, stride=2), :] = jnp.where(first, pltpu.roll(rows, BUCKET, 1), kinds)


def request(rows, kinds):
    return call(
        request_body,
        "request",
        [(shape(OWNERS, I32), VMEM)],
        [VMEM] * 2,
        [],
        WHOLE,
        moved=100_000,
    )(rows.reshape(-1, WIDTH), kinds.reshape(-1, WIDTH))[0]


def gather_tails_body(wanted, table, relations, out, factors_out, rows, factors, weighted, sems):
    copies = Copies(sems)
    for k in range(4):

        @pl.loop(k * OWNERS // 4, (k + 1) * OWNERS // 4)
        def _(b):
            base = b * LINE
            for i in range(BUCKET):
                rows[pl.ds(b * BUCKET + i, 1), :] = table[pl.ds(wanted[base + i], 1), :]
                row = wanted[base + BUCKET + i]
                factors[pl.ds(b * BUCKET + i, 1), :] = relations[pl.ds(row, 1), :]

        part = pl.ds(k * SLOTS // 4, SLOTS // 4)
        weighted[part, :] = (factors[part, :] * rows[part, :].astype(BF16).astype(F32)).astype(BF16)
        copies.start(weighted.at[part], out.at[part])
        copies.start(factors.at[part], factors_out.at[part])
    copies.wait()


def gather_tails(wanted, table, relations):
    return call(
        gather_tails_body,
        "gather_tails",
        [
            (shape(SLOTS, BF16), HBM),
            (shape(SLOTS, F32), HBM),
        ],
        [SMEM, VMEM, VMEM],
        [TABLE, TABLE, pltpu.VMEM((SLOTS, WIDTH), BF16), pltpu.SemaphoreType.DMA((8,))],
        WHOLE,
        flops=10_000_000_000,
        moved=20_000_000,
    )(wanted, table, relations)


def gather_own_body(place, src, table, out, rows, held, sems):
    copies = Copies(sems)
    head_rows(place, src, table, rows, (0,))
    held[...] = rows[...].astype(BF16)
    copies.start(held, out)
    copies.wait()


def gather_own(place, src, table):
    return call(
        gather_own_body,
        "gather_own",
        [(shape(EDGES, BF16), HBM)],
        [SMEM, SMEM, VMEM],
        [
            pltpu.VMEM((EDGES, WIDTH), F32),
            pltpu.VMEM((EDGES, WIDTH), BF16),
            pltpu.SemaphoreType.DMA((1,)),
        ],
        WHOLE,
        flops=3_000_000_000,
        moved=3_000_000,
    )(place, src, table)[0]


def edge_scores_body(
    place, counts, weighted_in, h0, n0, dr, vr, dl, vl, wr, wl, pulled_out, own, right, left, *rest
):
    weighted, heads, corrupt, grad_scores, pulled, o, r, l, in_sems, sems = rest
    owner = [(place[0] + COLS - s) & (COLS - 1) for s in range(COLS)]
    span = [slice(s * WIDTH, (s + 1) * WIDTH) for s in range(COLS)]
    arrivals, copies = Copies(in_sems), Copies(sems)

    def fetch(source, begin, target, row, s, n):
        return arrivals.start(source.at[pl.ds(begin, n)], target.at[pl.ds(row, n), pl.ds(s * WIDTH, WIDTH)])

    buckets = BLOCK // PART
    blocks = [pl.ds(k * buckets, buckets) for k in range(EDGES // BLOCK)]
    for_scores = [
        fetch(n0, 0, corrupt, 0, 0, NEG_PAD),
        fetch(vr, HALF, corrupt, 0, 1, HALF),
        fetch(dr, EDGES, corrupt, HALF, 1, HALF),
        fetch(wr, HALF, corrupt, 0, 2, HALF),
        fetch(wl, HALF, corrupt, HALF, 2, HALF),
        fetch(dl, EDGES, corrupt, 0, 3, HALF),
        fetch(vl, HALF, corrupt, HALF, 3, HALF),
    ]
    for_weights = [arrivals.start(weighted_in.at[at], weighted.at[at]) for at in blocks]
    for_heads = [
        fetch(h0, 0, heads, 0, 0, EDGES),
        fetch(dr, 0, heads, 0, 1, EDGES),
        fetch(wr, 0, heads, 0, 2, HALF),
        fetch(wl, 0, heads, HALF, 2, HALF),
        fetch(dl, 0, heads, 0, 3, EDGES),
    ]
    for copy in for_scores:
        copy.wait()

    def send(values, at, where, second):
        n = values.shape[0]
        via, via_out = (l, left) if second else (r, right)
        for s, held, out, begins in ((2, via, via_out, where), (1, l, left, at), (3, r, right, at), (0, o, own, at)):
            held[begins : begins + n, :] = values[:, span[s]]
            copies.start(held.at[pl.ds(begins, n)], out.at[pl.ds(begins, n)])

    negatives = corrupt[...]
    slot = lax.broadcasted_iota(I32, (PART, 1), 0) + place[0] * PART
    whole = []
    for k in range(EDGES // BLOCK):
        rows = slice(k * BLOCK, (k + 1) * BLOCK)
        live = jnp.concatenate(
            [(slot < counts[0, b]).astype(F32) for b in range(k * buckets, (k + 1) * buckets)], axis=0
        )
        for_weights[k].wait()
        wk = jnp.concatenate(
            [weighted[k * buckets : (k + 1) * buckets, owner[s]].reshape(BLOCK, WIDTH) for s in range(COLS)],
            axis=1,
        )
        whole.append(wk)
        scores = lax.dot_general(wk, negatives, (((1,), (1,)), ((), ())), preferred_element_type=F32)
        if k == 0:
            for copy in for_heads:
                copy.wait()
        wf, hf = wk.astype(F32), heads[rows, :].astype(F32)
        positive = jnp.sum(hf * wf, axis=1, keepdims=True)
        grad_positive = -live * jax.nn.sigmoid(-positive)
        grad = (live * jax.nn.sigmoid(scores) * (1.0 / NEG)).astype(BF16)
        grad_scores[rows, :] = grad
        total = jnp.dot(grad, negatives, preferred_element_type=F32) + grad_positive * hf
        total = total.astype(BF16)
        at = blocks[k]
        for s in range(COLS):
            pulled[at, owner[s]] = total[:, span[s]].reshape(buckets, PART, WIDTH)
        copies.start(pulled.at[at], pulled_out.at[at])
        send((grad_positive * wf).astype(BF16), k * BLOCK, DIRECT + k * BLOCK % HALF, k * BLOCK >= HALF)
    weights = jnp.concatenate(whole, axis=0)
    for k in range(NEG_PAD // BLOCK):
        total = lax.dot_general(
            grad_scores[:, k * BLOCK : (k + 1) * BLOCK],
            weights,
            (((0,), (0,)), ((), ())),
            preferred_element_type=F32,
        )
        send(
            total.astype(BF16),
            EDGES + k * BLOCK,
            DIRECT + HALF + k * BLOCK % HALF,
            k * BLOCK >= HALF,
        )
    copies.wait()


def edge_scores(place, counts, weighted, pieces):
    whole = (OWNERS, COLS, PART, WIDTH)
    sizes = (DIRECT, DIRECT + 2 * HALF, DIRECT + 2 * HALF)
    return call(
        edge_scores_body,
        "edge_scores",
        [(jax.ShapeDtypeStruct(whole, BF16), HBM)] + [(shape(n, BF16), HBM) for n in sizes],
        [SMEM, SMEM] + [HBM] * 9,
        [
            pltpu.VMEM(whole, BF16),
            pltpu.VMEM((EDGES, FULL), BF16),
            pltpu.VMEM((NEG_PAD, FULL), BF16),
            pltpu.VMEM((EDGES, NEG_PAD), BF16),
            pltpu.VMEM(whole, BF16),
        ]
        + [pltpu.VMEM((n, WIDTH), BF16) for n in sizes]
        + [pltpu.SemaphoreType.DMA((16,)), pltpu.SemaphoreType.DMA((36,))],
        WHOLE,
        flops=3_200_000_000,
        moved=8_000_000,
    )(place, counts, weighted, *pieces)


def begin(tables, start=None):
    for n, table in enumerate(tables):
        if n > 0 or start is None:
            table[...] = jnp.zeros((SLOTS, WIDTH), F32)
        else:
            table[...] = start[...]


def finish(tables):
    total = tables[0][...]
    for table in tables[1:]:
        total += table[...]
    tables[0][...] = total


def scatter_near_body(col, src, g0, g1, g3, out, b0, b1, b3, r0, r1, r3, sems, *tables):
    tables = (out,) + tables
    copies = Copies(sems)
    for source, target in ((g0, b0), (g1, b1), (g3, b3)):
        copies.start(source.at[pl.ds(0, EDGES)], target)
    begin(tables)
    copies.wait()
    for source, target in ((b0, r0), (b1, r1), (b3, r3)):
        target[...] = source[...].astype(F32)

    @pl.loop(0, OWNERS)
    def _(b):
        for i in range(PART):
            for s, rows in ((0, r0), (1, r1), (3, r3)):
                base = b * BUCKET + ((col[0] + s) & (COLS - 1)) * PART
                into = tables[(i * 3 + s) % CHAINS]
                into[pl.ds(src[base + i], 1), :] += rows[pl.ds(b * PART + i, 1), :]

    finish(tables)


def scatter_near(col, src, g0, g1, g3):
    return call(
        scatter_near_body,
        "scatter_near",
        [(shape(SLOTS, F32), VMEM)],
        [SMEM] * 2 + [HBM] * 3,
        [pltpu.VMEM((EDGES, WIDTH), BF16)] * 3
        + [pltpu.VMEM((EDGES, WIDTH), F32)] * 3
        + [pltpu.SemaphoreType.DMA((3,))]
        + [TABLE] * (CHAINS - 1),
        WHOLE,
        flops=10_000_000_000,
        moved=20_000_000,
    )(col, src, g0, g1, g3)[0]


def scatter_far_body(col, src, neg, start, g0, g1, g3, wr, wl, out, b0, b1, b3, br, bl, rr, rl, corrupt, sems, *tables):
    tables = (out,) + tables
    copies = Copies(sems)
    copies.start(wr, br)
    copies.start(wl, bl)
    for source, target in ((g0, b0), (g1, b1), (g3, b3)):
        copies.start(source.at[pl.ds(EDGES, NEG_PAD)], target)
    begin(tables, start)
    copies.wait()
    rr[...] = br[0:HALF, :].astype(F32)
    rl[...] = bl[0:HALF, :].astype(F32)
    near = b0[...].astype(F32) + b1[...].astype(F32) + b3[...].astype(F32)
    corrupt[0:HALF, :] = near[0:HALF, :] + br[HALF:, :].astype(F32)
    corrupt[HALF:, :] = near[HALF:, :] + bl[HALF:, :].astype(F32)

    @pl.loop(0, OWNERS // 2)
    def _(b):
        for i in range(PART):
            for n, rows in enumerate((rr, rl)):
                base = (b + n * OWNERS // 2) * BUCKET + ((col[0] + 2) & (COLS - 1)) * PART
                into = tables[(i * 2 + n) % CHAINS]
                into[pl.ds(src[base + i], 1), :] += rows[pl.ds(b * PART + i, 1), :]

    @pl.loop(0, NEG // 40)
    def _(g):
        for i in range(40):
            into = tables[i % CHAINS]
            into[pl.ds(neg[g * 40 + i], 1), :] += corrupt[pl.ds(g * 40 + i, 1), :]

    finish(tables)


def scatter_far(col, src, neg, start, g0, g1, g3, wr, wl):
    return call(
        scatter_far_body,
        "scatter_far",
        [(shape(SLOTS, F32), VMEM)],
        [SMEM] * 3 + [VMEM] + [HBM] * 5,
        [pltpu.VMEM((NEG_PAD, WIDTH), BF16)] * 5
        + [pltpu.VMEM((HALF, WIDTH), F32)] * 2
        + [pltpu.VMEM((NEG_PAD, WIDTH), F32), pltpu.SemaphoreType.DMA((5,))]
        + [TABLE] * (CHAINS - 1),
        WHOLE,
        flops=10_000_000_000,
        moved=20_000_000,
    )(col, src, neg, start, g0, g1, g3, wr, wl)[0]


def scatter_tails_body(wanted, start, factors, pulled, out, squares, held, scale, rows, first, in_sems, *tables):
    arrivals = Copies(in_sems)
    parts = [pl.ds(k * SLOTS // 4, SLOTS // 4) for k in range(4)]
    needed = [
        [arrivals.start(source.at[part], target.at[part]) for source, target in ((pulled, held), (factors, scale))]
        for part in parts
    ]
    last = arrivals.start(start, first)
    begin(tables)
    for k, part in enumerate(parts):
        for copy in needed[k]:
            copy.wait()
        rows[part, :] = scale[part, :] * held[part, :].astype(F32)

        @pl.loop(k * OWNERS // 4, (k + 1) * OWNERS // 4)
        def _(b):
            for i in range(BUCKET):
                into = tables[i % CHAINS]
                into[pl.ds(wanted[b * BUCKET + i], 1), :] += rows[pl.ds(b * BUCKET + i, 1), :]

    last.wait()
    ones = jnp.ones((16, 2 * WIDTH), BF16)
    for k, part in enumerate(parts):
        total = first[part, :]
        for table in tables:
            total += table[part, :]
        out[part, :] = total
        square = total * total
        high = square.astype(BF16)
        low = (square - high.astype(F32)).astype(BF16)
        sums = lax.dot_general(
            ones, jnp.concatenate([high, low], axis=1), (((1,), (1,)), ((), ())), preferred_element_type=F32
        )
        for n in range(SLOTS // 4 // WIDTH):
            line = k * SLOTS // 4 // WIDTH + n
            squares[line : line + 1, :] = sums[0:1, n * WIDTH : (n + 1) * WIDTH]


def scatter_tails(wanted, start, factors, pulled):
    return call(
        scatter_tails_body,
        "scatter_tails",
        [(shape(SLOTS, F32), VMEM), (shape(SLOTS // WIDTH, F32), VMEM)],
        [SMEM] + [HBM] * 3,
        [pltpu.VMEM((SLOTS, WIDTH), BF16), TABLE, TABLE, TABLE]
        + [pltpu.SemaphoreType.DMA((9,))]
        + [TABLE] * CHAINS,
        WHOLE,
        moved=30_000_000,
    )(wanted, start, factors, pulled)


def stage_body(table, gradient, table_out, step_out):
    table_out[...] = table[...]
    step_out[...] = gradient[...] * learning_rate


def stage(table, gradient):
    return call(
        stage_body,
        "stage",
        [(shape(SLOTS, F32), VMEM)] * 2,
        [VMEM] * 2,
        [],
        12 * 1024,
        moved=8_000_000,
    )(table, gradient)


def pass_on_body(g1, g3, out_r, out_l, r, l, in_sems, sems):
    arrivals, copies = Copies(in_sems), Copies(sems)
    arrivals.start(g3.at[pl.ds(DIRECT, 2 * HALF)], r)
    arrivals.start(g1.at[pl.ds(DIRECT, 2 * HALF)], l)
    arrivals.wait()
    copies.start(r, out_r)
    copies.start(l, out_l)
    copies.wait()


def pass_on(g1, g3):
    return call(
        pass_on_body,
        "pass_on",
        [(shape(2 * HALF, BF16), HBM)] * 2,
        [HBM] * 2,
        [pltpu.VMEM((2 * HALF, WIDTH), BF16)] * 2 + [pltpu.SemaphoreType.DMA((2,))] * 2,
        moved=1_000_000,
    )(g1, g3)


def shifted(x, s):
    return lax.ppermute(x, "col", [(i, (i + s) % COLS) for i in range(COLS)])


def shards(
    embeddings, adagrad_state, relations, src_rows, dst_rows, rel_ids, bucket_counts, neg_rows
):
    axes = ("dom", "col")
    place = lax.axis_index("col").astype(I32).reshape(1)

    def sent(x):
        return lax.all_to_all(
            x.reshape(OWNERS * COLS, PART, WIDTH), axes, split_axis=0, concat_axis=0, tiled=True
        )

    words = request(dst_rows, rel_ids)
    wanted = lax.all_to_all(words, "dom", split_axis=0, concat_axis=0, tiled=True)
    via_r, via_l, negatives = gather_far(place, src_rows, neg_rows, embeddings)
    vr, vl = shifted(via_r, 1), shifted(via_l, -1)
    weighted, factors = gather_tails(wanted.reshape(-1), embeddings, relations)
    weighted = sent(weighted).reshape(OWNERS, COLS, PART, WIDTH)
    after, factors, vr, vl = lax.optimization_barrier((negatives, factors, vr, vl))
    right, left = gather_near(place, src_rows, embeddings, after)
    near_r, near_l = shifted(right, 1), shifted(left, -1)
    wr, wl = shifted(vr, 1), shifted(vl, -1)
    own_rows, wr, wl = lax.optimization_barrier((src_rows, wr, wl))
    heads = gather_own(place, own_rows, embeddings)
    pieces = [heads, after, near_r, vr, near_l, vl, wr, wl]
    pulled, own, right, left = edge_scores(place, bucket_counts, weighted, pieces)
    pulled = sent(pulled).reshape(SLOTS, WIDTH)
    from_left, from_right = shifted(right, 1), shifted(left, -1)
    on_r, on_l = pass_on(from_right, from_left)
    far_a, far_b = shifted(on_r, 1), shifted(on_l, -1)
    gradient = scatter_near(place, src_rows, own, from_right, from_left)
    gradient = scatter_far(place, src_rows, neg_rows, gradient, own, from_right, from_left, far_a, far_b)
    gradient, squares = scatter_tails(
        wanted[:, :BUCKET].reshape(-1), gradient, factors, pulled
    )

    table, step = stage(embeddings, gradient)
    squares = (squares + shifted(squares, 2)) + (shifted(squares, 1) + shifted(squares, 3))
    new_state = adagrad_state + squares.reshape(-1) / FULL
    new_embeddings = table - step / jnp.sqrt(new_state)[:, None]
    return (new_embeddings, new_state)


def solution(mesh):
    placed = (
        P("dom", "col"),
        P("dom"),
        P(None, "col"),
        P("dom"),
        P("dom"),
        P("dom"),
        P("dom", None),
        P("dom"),
    )
    return jax.shard_map(
        shards, mesh=mesh, in_specs=placed, out_specs=(P("dom", "col"), P("dom")), check_vma=False
    )
```

```python
import jax
import jax.numpy as jnp
from jax import lax
from jax.experimental import pallas as pl
from jax.experimental.pallas import tpu as pltpu
from jax.sharding import PartitionSpec as P

learning_rate = 0.3
OWNERS = 64
COLS = 4
PART = 16
BUCKET = COLS * PART
SLOTS = OWNERS * BUCKET
EDGES = OWNERS * PART
WIDTH = 128
FULL = COLS * WIDTH
NEG = 1000
NEG_PAD = 1024
DIRECT = EDGES + NEG_PAD
BUCKETS_END = OWNERS
HALF = 512
BLOCK = 256
CHAINS = 8
WHOLE = 65_300
WORDS_STAY = 54_528

F32, BF16, I32 = jnp.float32, jnp.bfloat16, jnp.int32
SMEM = pl.BlockSpec(memory_space=pltpu.SMEM)
VMEM = pl.BlockSpec(memory_space=pltpu.VMEM)
HBM = pl.BlockSpec(memory_space=pltpu.HBM)
TABLE = pltpu.VMEM((SLOTS, WIDTH), F32)


def call(body, name, outs, ins, scratch, kib=WHOLE, flops=0, moved=0):
    return pl.pallas_call(
        body,
        out_shape=[shape for shape, _ in outs],
        in_specs=ins,
        out_specs=[spec for _, spec in outs],
        scratch_shapes=scratch,
        compiler_params=pltpu.CompilerParams(vmem_limit_bytes=kib * 1024),
        cost_estimate=pl.CostEstimate(flops=flops, bytes_accessed=moved, transcendentals=0),
        name=name,
    )


def shape(rows, dtype, width=WIDTH):
    return jax.ShapeDtypeStruct((rows, width), dtype)


def rows_at(start, count):
    return pl.ds(start, count)


class Copies:
    def __init__(self, sems):
        self.sems, self.all = sems, []

    def start(self, source, target):
        self.all.append(pltpu.make_async_copy(source, target, self.sems.at[len(self.all)]))
        self.all[-1].start()
        return self.all[-1]

    def wait(self):
        for copy in self.all:
            copy.wait()


def head_rows(place, src, table, rows, pieces):
    @pl.loop(0, OWNERS)
    def _(b):
        for n, s in enumerate(pieces):
            base = b * BUCKET + ((place[0] + s) & (COLS - 1)) * PART
            for i in range(PART):
                rows[pl.ds(n * EDGES + b * PART + i, 1), :] = table[pl.ds(src[base + i], 1), :]


def gather_far_body(place, src, neg, table, via_r, via_l, corrupt_out, rows, corrupt, rounded, vr, vl, sems):
    copies = Copies(sems)

    @pl.loop(0, NEG // 40)
    def _(g):
        for i in range(40):
            corrupt[pl.ds(g * 40 + i, 1), :] = table[pl.ds(neg[g * 40 + i], 1), :]

    corrupt[NEG:NEG_PAD, :] = jnp.zeros((NEG_PAD - NEG, WIDTH), F32)
    rounded[...] = corrupt[...].astype(BF16)
    copies.start(rounded, corrupt_out)
    head_rows(place, src, table, rows, (2,))
    for held, out, part in ((vr, via_r, slice(0, HALF)), (vl, via_l, slice(HALF, 2 * HALF))):
        held[0:HALF, :] = rows[part, :].astype(BF16)
        held[HALF:, :] = rounded[part, :]
        copies.start(held, out)
    copies.wait()


def gather_far(place, src, neg, table):
    return call(
        gather_far_body,
        "gather_far",
        [(shape(2 * HALF, BF16), HBM)] * 3,
        [SMEM, SMEM, SMEM, VMEM],
        [pltpu.VMEM((EDGES, WIDTH), F32), pltpu.VMEM((NEG_PAD, WIDTH), F32)]
        + [pltpu.VMEM((2 * HALF, WIDTH), BF16)] * 3
        + [pltpu.SemaphoreType.DMA((3,))],
        WHOLE,
        moved=10_000_000,
    )(place, src, neg, table)


def gather_near_body(place, src, table, corrupt, right, left, rows, halves, r, l, in_sems, sems):
    arrivals, copies = Copies(in_sems), Copies(sems)
    arrivals.start(corrupt, halves)
    head_rows(place, src, table, rows, (1, 3))
    arrivals.wait()
    r[0:EDGES, :] = rows[0:EDGES, :].astype(BF16)
    r[EDGES:, :] = halves[HALF:, :]
    copies.start(r, right)
    l[0:EDGES, :] = rows[EDGES : 2 * EDGES, :].astype(BF16)
    l[EDGES:, :] = halves[0:HALF, :]
    copies.start(l, left)
    copies.wait()


def gather_near(place, src, table, corrupt):
    sizes = (EDGES + HALF, EDGES + HALF)
    return call(
        gather_near_body,
        "gather_near",
        [(shape(n, BF16), HBM) for n in sizes],
        [SMEM, SMEM, VMEM, HBM],
        [pltpu.VMEM((2 * EDGES, WIDTH), F32), pltpu.VMEM((NEG_PAD, WIDTH), BF16)]
        + [pltpu.VMEM((n, WIDTH), BF16) for n in sizes]
        + [pltpu.SemaphoreType.DMA((1,)), pltpu.SemaphoreType.DMA((2,))],
        WHOLE,
        flops=17_000_000_000,
        moved=20_000_000,
    )(place, src, table, corrupt)


LINE = 2 * BUCKET


def request_body(rows, kinds, out):
    first = lax.broadcasted_iota(I32, (OWNERS // 2, WIDTH), 1) < BUCKET
    rows, kinds = rows[...], kinds[...]
    out[pl.ds(0, OWNERS // 2, stride=2), :] = jnp.where(first, rows, pltpu.roll(kinds, BUCKET, 1))
    out[pl.ds(1, OWNERS // 2, stride=2), :] = jnp.where(first, pltpu.roll(rows, BUCKET, 1), kinds)


def request(rows, kinds):
    return call(
        request_body,
        "request",
        [(shape(OWNERS, I32), VMEM)],
        [VMEM] * 2,
        [],
        WHOLE,
        moved=100_000,
    )(rows.reshape(-1, WIDTH), kinds.reshape(-1, WIDTH))[0]


def gather_tails_body(
    wanted_in, table_in, relations_in, out, factors_out, wanted, table, relations, rows, factors, weighted, in_sems, sems
):
    arrivals, copies = Copies(in_sems), Copies(sems)
    arrivals.start(wanted_in, wanted)
    arrivals.start(relations_in, relations)
    last = arrivals.start(table_in, table)
    for copy in arrivals.all[:2]:
        copy.wait()

    def factor(b, i):
        row = wanted[b * LINE + BUCKET + i]
        factors[pl.ds(b * BUCKET + i, 1), :] = relations[pl.ds(row, 1), :]

    for k in range(4):
        if k == 0:

            @pl.loop(0, OWNERS // 4)
            def _(b):
                for i in range(BUCKET):
                    factor(b, i)

            last.wait()

        @pl.loop(k * OWNERS // 4, (k + 1) * OWNERS // 4)
        def _(b):
            for i in range(BUCKET):
                rows[pl.ds(b * BUCKET + i, 1), :] = table[pl.ds(wanted[b * LINE + i], 1), :]
                if k > 0:
                    factor(b, i)

        part = pl.ds(k * SLOTS // 4, SLOTS // 4)
        weighted[part, :] = (factors[part, :] * rows[part, :].astype(BF16).astype(F32)).astype(BF16)
        copies.start(weighted.at[part], out.at[part])
        copies.start(factors.at[part], factors_out.at[part])
    copies.wait()


def gather_tails(wanted, table, relations):
    return call(
        gather_tails_body,
        "gather_tails",
        [
            (shape(SLOTS, BF16), HBM),
            (shape(SLOTS, F32), HBM),
        ],
        [HBM] * 3,
        [pltpu.SMEM(wanted.shape, I32), TABLE, pltpu.VMEM(relations.shape, F32), TABLE, TABLE]
        + [pltpu.VMEM((SLOTS, WIDTH), BF16), pltpu.SemaphoreType.DMA((3,)), pltpu.SemaphoreType.DMA((8,))],
        WORDS_STAY,
        flops=10_000_000_000,
        moved=20_000_000,
    )(wanted, table, relations)


def gather_own_body(place, src, table, out, rows, held, sems):
    copies = Copies(sems)
    head_rows(place, src, table, rows, (0,))
    held[...] = rows[...].astype(BF16)
    copies.start(held, out)
    copies.wait()


def gather_own(place, src, table):
    return call(
        gather_own_body,
        "gather_own",
        [(shape(EDGES, BF16), HBM)],
        [SMEM, SMEM, VMEM],
        [
            pltpu.VMEM((EDGES, WIDTH), F32),
            pltpu.VMEM((EDGES, WIDTH), BF16),
            pltpu.SemaphoreType.DMA((1,)),
        ],
        WHOLE,
        flops=3_000_000_000,
        moved=3_000_000,
    )(place, src, table)[0]


def edge_scores_body(
    settings_in, weighted_in, h0, n0, dr, vr, dl, vl, wr, wl, pulled_out, own, right, left, *rest
):
    settings, weighted, heads, corrupt, grad_scores, pulled, o, r, l, in_sems, sems = rest
    span = [slice(s * WIDTH, (s + 1) * WIDTH) for s in range(COLS)]
    arrivals, copies = Copies(in_sems), Copies(sems)
    for_masks = arrivals.start(settings_in, settings)

    def fetch(source, begin, target, row, s, n):
        return arrivals.start(source.at[pl.ds(begin, n)], target.at[pl.ds(row, n), pl.ds(s * WIDTH, WIDTH)])

    buckets = BLOCK // PART
    blocks = [pl.ds(k * buckets, buckets) for k in range(EDGES // BLOCK)]
    for_scores = [
        fetch(n0, 0, corrupt, 0, 0, NEG_PAD),
        fetch(vr, HALF, corrupt, 0, 1, HALF),
        fetch(dr, EDGES, corrupt, HALF, 1, HALF),
        fetch(wr, HALF, corrupt, 0, 2, HALF),
        fetch(wl, HALF, corrupt, HALF, 2, HALF),
        fetch(dl, EDGES, corrupt, 0, 3, HALF),
        fetch(vl, HALF, corrupt, HALF, 3, HALF),
    ]
    for_weights = [arrivals.start(weighted_in.at[at], weighted.at[at]) for at in blocks]
    for_heads = [
        fetch(h0, 0, heads, 0, 0, EDGES),
        fetch(dr, 0, heads, 0, 1, EDGES),
        fetch(wr, 0, heads, 0, 2, HALF),
        fetch(wl, 0, heads, HALF, 2, HALF),
        fetch(dl, 0, heads, 0, 3, EDGES),
    ]
    for_masks.wait()
    place = settings[0, BUCKETS_END]
    owner = [(place + COLS - s) & (COLS - 1) for s in range(COLS)]
    for copy in for_scores:
        copy.wait()

    def send(values, at, where, second):
        n = values.shape[0]
        via, via_out = (l, left) if second else (r, right)
        for s, held, out, begins in ((2, via, via_out, where), (1, l, left, at), (3, r, right, at), (0, o, own, at)):
            held[begins : begins + n, :] = values[:, span[s]]
            copies.start(held.at[pl.ds(begins, n)], out.at[pl.ds(begins, n)])

    negatives = corrupt[...]
    slot = lax.broadcasted_iota(I32, (PART, 1), 0) + place * PART
    whole = []
    for k in range(EDGES // BLOCK):
        rows = slice(k * BLOCK, (k + 1) * BLOCK)
        live = jnp.concatenate(
            [(slot < settings[0, b]).astype(F32) for b in range(k * buckets, (k + 1) * buckets)], axis=0
        )
        for_weights[k].wait()
        wk = jnp.concatenate(
            [weighted[k * buckets : (k + 1) * buckets, owner[s]].reshape(BLOCK, WIDTH) for s in range(COLS)],
            axis=1,
        )
        whole.append(wk)
        scores = lax.dot_general(wk, negatives, (((1,), (1,)), ((), ())), preferred_element_type=F32)
        if k == 0:
            for copy in for_heads:
                copy.wait()
        wf, hf = wk.astype(F32), heads[rows, :].astype(F32)
        positive = jnp.sum(hf * wf, axis=1, keepdims=True)
        grad_positive = -live * jax.nn.sigmoid(-positive)
        grad = (live * jax.nn.sigmoid(scores) * (1.0 / NEG)).astype(BF16)
        grad_scores[rows, :] = grad
        total = jnp.dot(grad, negatives, preferred_element_type=F32) + grad_positive * hf
        total = total.astype(BF16)
        at = blocks[k]
        for s in range(COLS):
            pulled[at, owner[s]] = total[:, span[s]].reshape(buckets, PART, WIDTH)
        copies.start(pulled.at[at], pulled_out.at[at])
        send((grad_positive * wf).astype(BF16), k * BLOCK, DIRECT + k * BLOCK % HALF, k * BLOCK >= HALF)
    weights = jnp.concatenate(whole, axis=0)
    for k in range(NEG_PAD // BLOCK):
        total = lax.dot_general(
            grad_scores[:, k * BLOCK : (k + 1) * BLOCK],
            weights,
            (((0,), (0,)), ((), ())),
            preferred_element_type=F32,
        )
        send(
            total.astype(BF16),
            EDGES + k * BLOCK,
            DIRECT + HALF + k * BLOCK % HALF,
            k * BLOCK >= HALF,
        )
    copies.wait()


def edge_scores(settings, weighted, pieces):
    whole = (OWNERS, COLS, PART, WIDTH)
    sizes = (DIRECT, DIRECT + 2 * HALF, DIRECT + 2 * HALF)
    return call(
        edge_scores_body,
        "edge_scores",
        [(jax.ShapeDtypeStruct(whole, BF16), HBM)] + [(shape(n, BF16), HBM) for n in sizes],
        [HBM] * 10,
        [
            pltpu.SMEM(settings.shape, I32),
            pltpu.VMEM(whole, BF16),
            pltpu.VMEM((EDGES, FULL), BF16),
            pltpu.VMEM((NEG_PAD, FULL), BF16),
            pltpu.VMEM((EDGES, NEG_PAD), BF16),
            pltpu.VMEM(whole, BF16),
        ]
        + [pltpu.VMEM((n, WIDTH), BF16) for n in sizes]
        + [pltpu.SemaphoreType.DMA((17,)), pltpu.SemaphoreType.DMA((36,))],
        WHOLE,
        flops=3_200_000_000,
        moved=8_000_000,
    )(settings, weighted, *pieces)


def begin(tables, start=None):
    for n, table in enumerate(tables):
        if n > 0 or start is None:
            table[...] = jnp.zeros((SLOTS, WIDTH), F32)
        else:
            table[...] = start[...]


def finish(tables):
    total = tables[0][...]
    for table in tables[1:]:
        total += table[...]
    tables[0][...] = total


def scatter_near_body(col, src, g0, g1, g3, out, b0, b1, b3, r0, r1, r3, sems, *tables):
    tables = (out,) + tables
    copies = Copies(sems)
    for source, target in ((g0, b0), (g1, b1), (g3, b3)):
        copies.start(source.at[pl.ds(0, EDGES)], target)
    begin(tables)
    copies.wait()
    for source, target in ((b0, r0), (b1, r1), (b3, r3)):
        target[...] = source[...].astype(F32)

    @pl.loop(0, OWNERS)
    def _(b):
        for i in range(PART):
            for s, rows in ((0, r0), (1, r1), (3, r3)):
                base = b * BUCKET + ((col[0] + s) & (COLS - 1)) * PART
                into = tables[(i * 3 + s) % CHAINS]
                into[pl.ds(src[base + i], 1), :] += rows[pl.ds(b * PART + i, 1), :]

    finish(tables)


def scatter_near(col, src, g0, g1, g3):
    return call(
        scatter_near_body,
        "scatter_near",
        [(shape(SLOTS, F32), VMEM)],
        [SMEM] * 2 + [HBM] * 3,
        [pltpu.VMEM((EDGES, WIDTH), BF16)] * 3
        + [pltpu.VMEM((EDGES, WIDTH), F32)] * 3
        + [pltpu.SemaphoreType.DMA((3,))]
        + [TABLE] * (CHAINS - 1),
        WHOLE,
        flops=10_000_000_000,
        moved=20_000_000,
    )(col, src, g0, g1, g3)[0]


def scatter_far_body(col, src, neg, start, g0, g1, g3, wr, wl, out, b0, b1, b3, br, bl, rr, rl, corrupt, sems, *tables):
    tables = (out,) + tables
    copies = Copies(sems)
    copies.start(wr, br)
    copies.start(wl, bl)
    for source, target in ((g0, b0), (g1, b1), (g3, b3)):
        copies.start(source.at[pl.ds(EDGES, NEG_PAD)], target)
    begin(tables, start)
    copies.wait()
    rr[...] = br[0:HALF, :].astype(F32)
    rl[...] = bl[0:HALF, :].astype(F32)
    near = b0[...].astype(F32) + b1[...].astype(F32) + b3[...].astype(F32)
    corrupt[0:HALF, :] = near[0:HALF, :] + br[HALF:, :].astype(F32)
    corrupt[HALF:, :] = near[HALF:, :] + bl[HALF:, :].astype(F32)

    @pl.loop(0, OWNERS // 2)
    def _(b):
        for i in range(PART):
            for n, rows in enumerate((rr, rl)):
                base = (b + n * OWNERS // 2) * BUCKET + ((col[0] + 2) & (COLS - 1)) * PART
                into = tables[(i * 2 + n) % CHAINS]
                into[pl.ds(src[base + i], 1), :] += rows[pl.ds(b * PART + i, 1), :]

    @pl.loop(0, NEG // 40)
    def _(g):
        for i in range(40):
            into = tables[i % CHAINS]
            into[pl.ds(neg[g * 40 + i], 1), :] += corrupt[pl.ds(g * 40 + i, 1), :]

    finish(tables)


def scatter_far(col, src, neg, start, g0, g1, g3, wr, wl):
    return call(
        scatter_far_body,
        "scatter_far",
        [(shape(SLOTS, F32), VMEM)],
        [SMEM] * 3 + [VMEM] + [HBM] * 5,
        [pltpu.VMEM((NEG_PAD, WIDTH), BF16)] * 5
        + [pltpu.VMEM((HALF, WIDTH), F32)] * 2
        + [pltpu.VMEM((NEG_PAD, WIDTH), F32), pltpu.SemaphoreType.DMA((5,))]
        + [TABLE] * (CHAINS - 1),
        WHOLE,
        flops=10_000_000_000,
        moved=20_000_000,
    )(col, src, neg, start, g0, g1, g3, wr, wl)[0]


def scatter_tails_body(
    wanted_in, start, factors, pulled, out, squares, wanted, held, scale, rows, first, in_sems, *tables
):
    arrivals = Copies(in_sems)
    for_rows = arrivals.start(wanted_in, wanted)
    parts = [pl.ds(k * SLOTS // 4, SLOTS // 4) for k in range(4)]
    needed = [
        [arrivals.start(source.at[part], target.at[part]) for source, target in ((pulled, held), (factors, scale))]
        for part in parts
    ]
    last = arrivals.start(start, first)
    begin(tables)
    for_rows.wait()
    for k, part in enumerate(parts):
        for copy in needed[k]:
            copy.wait()
        rows[part, :] = scale[part, :] * held[part, :].astype(F32)

        @pl.loop(k * OWNERS // 4, (k + 1) * OWNERS // 4)
        def _(b):
            for i in range(BUCKET):
                into = tables[i % CHAINS]
                into[pl.ds(wanted[b * BUCKET + i], 1), :] += rows[pl.ds(b * BUCKET + i, 1), :]

    last.wait()
    ones = jnp.ones((16, 2 * WIDTH), BF16)
    for k, part in enumerate(parts):
        total = first[part, :]
        for table in tables:
            total += table[part, :]
        out[part, :] = total
        square = total * total
        high = square.astype(BF16)
        low = (square - high.astype(F32)).astype(BF16)
        sums = lax.dot_general(
            ones, jnp.concatenate([high, low], axis=1), (((1,), (1,)), ((), ())), preferred_element_type=F32
        )
        for n in range(SLOTS // 4 // WIDTH):
            line = k * SLOTS // 4 // WIDTH + n
            squares[line : line + 1, :] = sums[0:1, n * WIDTH : (n + 1) * WIDTH]


def scatter_tails(wanted, start, factors, pulled):
    return call(
        scatter_tails_body,
        "scatter_tails",
        [(shape(SLOTS, F32), VMEM), (shape(SLOTS // WIDTH, F32), VMEM)],
        [HBM] * 4,
        [pltpu.SMEM((SLOTS,), I32), pltpu.VMEM((SLOTS, WIDTH), BF16), TABLE, TABLE, TABLE]
        + [pltpu.SemaphoreType.DMA((10,))]
        + [TABLE] * CHAINS,
        WHOLE,
        moved=30_000_000,
    )(wanted, start, factors, pulled)


def stage_body(table, gradient, table_out, step_out):
    table_out[...] = table[...]
    step_out[...] = gradient[...] * learning_rate


def stage(table, gradient):
    return call(
        stage_body,
        "stage",
        [(shape(SLOTS, F32), VMEM)] * 2,
        [VMEM] * 2,
        [],
        12 * 1024,
        moved=8_000_000,
    )(table, gradient)


def pass_on_body(g1, g3, out_r, out_l, r, l, in_sems, sems):
    arrivals, copies = Copies(in_sems), Copies(sems)
    arrivals.start(g3.at[pl.ds(DIRECT, 2 * HALF)], r)
    arrivals.start(g1.at[pl.ds(DIRECT, 2 * HALF)], l)
    arrivals.wait()
    copies.start(r, out_r)
    copies.start(l, out_l)
    copies.wait()


def pass_on(g1, g3):
    return call(
        pass_on_body,
        "pass_on",
        [(shape(2 * HALF, BF16), HBM)] * 2,
        [HBM] * 2,
        [pltpu.VMEM((2 * HALF, WIDTH), BF16)] * 2 + [pltpu.SemaphoreType.DMA((2,))] * 2,
        moved=1_000_000,
    )(g1, g3)


def shifted(x, s):
    return lax.ppermute(x, "col", [(i, (i + s) % COLS) for i in range(COLS)])


def shards(
    embeddings, adagrad_state, relations, src_rows, dst_rows, rel_ids, bucket_counts, neg_rows
):
    axes = ("dom", "col")
    place = lax.axis_index("col").astype(I32).reshape(1)
    settings = jnp.concatenate([bucket_counts, jnp.broadcast_to(place, bucket_counts.shape)], axis=1)

    def sent(x):
        return lax.all_to_all(
            x.reshape(OWNERS * COLS, PART, WIDTH), axes, split_axis=0, concat_axis=0, tiled=True
        )

    words = request(dst_rows, rel_ids)
    wanted = lax.all_to_all(words, "dom", split_axis=0, concat_axis=0, tiled=True)
    via_r, via_l, negatives = gather_far(place, src_rows, neg_rows, embeddings)
    vr, vl = shifted(via_r, 1), shifted(via_l, -1)
    weighted, factors = gather_tails(wanted.reshape(-1), embeddings, relations)
    weighted = sent(weighted).reshape(OWNERS, COLS, PART, WIDTH)
    after, factors, vr, vl = lax.optimization_barrier((negatives, factors, vr, vl))
    right, left = gather_near(place, src_rows, embeddings, after)
    near_r, near_l = shifted(right, 1), shifted(left, -1)
    wr, wl = shifted(vr, 1), shifted(vl, -1)
    own_rows, wr, wl = lax.optimization_barrier((src_rows, wr, wl))
    heads = gather_own(place, own_rows, embeddings)
    pieces = [heads, after, near_r, vr, near_l, vl, wr, wl]
    pulled, own, right, left = edge_scores(settings, weighted, pieces)
    pulled = sent(pulled).reshape(SLOTS, WIDTH)
    from_left, from_right = shifted(right, 1), shifted(left, -1)
    on_r, on_l = pass_on(from_right, from_left)
    far_a, far_b = shifted(on_r, 1), shifted(on_l, -1)
    gradient = scatter_near(place, src_rows, own, from_right, from_left)
    gradient = scatter_far(place, src_rows, neg_rows, gradient, own, from_right, from_left, far_a, far_b)
    gradient, squares = scatter_tails(
        wanted[:, :BUCKET].reshape(-1), gradient, factors, pulled
    )

    table, step = stage(embeddings, gradient)
    squares = (squares + shifted(squares, 2)) + (shifted(squares, 1) + shifted(squares, 3))
    new_state = adagrad_state + squares.reshape(-1) / FULL
    new_embeddings = table - step / jnp.sqrt(new_state)[:, None]
    return (new_embeddings, new_state)


def solution(mesh):
    placed = (
        P("dom", "col"),
        P("dom"),
        P(None, "col"),
        P("dom"),
        P("dom"),
        P("dom"),
        P("dom", None),
        P("dom"),
    )
    return jax.shard_map(
        shards, mesh=mesh, in_specs=placed, out_specs=(P("dom", "col"), P("dom")), check_vma=False
    )
```

```python
import jax
import jax.numpy as jnp
from jax import lax
from jax.experimental import pallas as pl
from jax.experimental.pallas import tpu as pltpu
from jax.sharding import PartitionSpec as P

learning_rate = 0.3
OWNERS = 64
COLS = 4
PART = 16
BUCKET = COLS * PART
SLOTS = OWNERS * BUCKET
EDGES = OWNERS * PART
WIDTH = 128
FULL = COLS * WIDTH
NEG = 1000
NEG_PAD = 1024
DIRECT = EDGES + NEG_PAD
BUCKETS_END = OWNERS
HALF = 512
BLOCK = 256
CHAINS = 8
WHOLE = 65_300
WORDS_STAY = 54_528

F32, BF16, I32 = jnp.float32, jnp.bfloat16, jnp.int32
SMEM = pl.BlockSpec(memory_space=pltpu.SMEM)
VMEM = pl.BlockSpec(memory_space=pltpu.VMEM)
HBM = pl.BlockSpec(memory_space=pltpu.HBM)
TABLE = pltpu.VMEM((SLOTS, WIDTH), F32)


def call(body, name, outs, ins, scratch, kib=WHOLE, flops=0, moved=0):
    return pl.pallas_call(
        body,
        out_shape=[shape for shape, _ in outs],
        in_specs=ins,
        out_specs=[spec for _, spec in outs],
        scratch_shapes=scratch,
        compiler_params=pltpu.CompilerParams(vmem_limit_bytes=kib * 1024),
        cost_estimate=pl.CostEstimate(flops=flops, bytes_accessed=moved, transcendentals=0),
        name=name,
    )


def shape(rows, dtype, width=WIDTH):
    return jax.ShapeDtypeStruct((rows, width), dtype)


def rows_at(start, count):
    return pl.ds(start, count)


class Copies:
    def __init__(self, sems):
        self.sems, self.all = sems, []

    def start(self, source, target):
        self.all.append(pltpu.make_async_copy(source, target, self.sems.at[len(self.all)]))
        self.all[-1].start()
        return self.all[-1]

    def wait(self):
        for copy in self.all:
            copy.wait()


def head_rows(place, src, table, rows, pieces):
    @pl.loop(0, OWNERS)
    def _(b):
        for n, s in enumerate(pieces):
            base = b * BUCKET + ((place[0] + s) & (COLS - 1)) * PART
            for i in range(PART):
                rows[pl.ds(n * EDGES + b * PART + i, 1), :] = table[pl.ds(src[base + i], 1), :]


def gather_far_body(place, src, neg, table, via_r, via_l, corrupt_out, rows, corrupt, rounded, vr, vl, sems):
    copies = Copies(sems)

    @pl.loop(0, NEG // 40)
    def _(g):
        for i in range(40):
            corrupt[pl.ds(g * 40 + i, 1), :] = table[pl.ds(neg[g * 40 + i], 1), :]

    corrupt[NEG:NEG_PAD, :] = jnp.zeros((NEG_PAD - NEG, WIDTH), F32)
    rounded[...] = corrupt[...].astype(BF16)
    copies.start(rounded, corrupt_out)
    head_rows(place, src, table, rows, (2,))
    for held, out, part in ((vr, via_r, slice(0, HALF)), (vl, via_l, slice(HALF, 2 * HALF))):
        held[0:HALF, :] = rows[part, :].astype(BF16)
        held[HALF:, :] = rounded[part, :]
        copies.start(held, out)
    copies.wait()


def gather_far(place, src, neg, table):
    return call(
        gather_far_body,
        "gather_far",
        [(shape(2 * HALF, BF16), HBM)] * 3,
        [SMEM, SMEM, SMEM, VMEM],
        [pltpu.VMEM((EDGES, WIDTH), F32), pltpu.VMEM((NEG_PAD, WIDTH), F32)]
        + [pltpu.VMEM((2 * HALF, WIDTH), BF16)] * 3
        + [pltpu.SemaphoreType.DMA((3,))],
        WHOLE,
        moved=10_000_000,
    )(place, src, neg, table)


def gather_near_body(place, src, table, corrupt, right, left, rows, halves, r, l, in_sems, sems):
    arrivals, copies = Copies(in_sems), Copies(sems)
    arrivals.start(corrupt, halves)
    head_rows(place, src, table, rows, (1, 3))
    arrivals.wait()
    r[0:EDGES, :] = rows[0:EDGES, :].astype(BF16)
    r[EDGES:, :] = halves[HALF:, :]
    copies.start(r, right)
    l[0:EDGES, :] = rows[EDGES : 2 * EDGES, :].astype(BF16)
    l[EDGES:, :] = halves[0:HALF, :]
    copies.start(l, left)
    copies.wait()


def gather_near(place, src, table, corrupt):
    sizes = (EDGES + HALF, EDGES + HALF)
    return call(
        gather_near_body,
        "gather_near",
        [(shape(n, BF16), HBM) for n in sizes],
        [SMEM, SMEM, VMEM, HBM],
        [pltpu.VMEM((2 * EDGES, WIDTH), F32), pltpu.VMEM((NEG_PAD, WIDTH), BF16)]
        + [pltpu.VMEM((n, WIDTH), BF16) for n in sizes]
        + [pltpu.SemaphoreType.DMA((1,)), pltpu.SemaphoreType.DMA((2,))],
        WHOLE,
        flops=17_000_000_000,
        moved=20_000_000,
    )(place, src, table, corrupt)


LINE = 2 * BUCKET


def request_body(rows, kinds, out):
    first = lax.broadcasted_iota(I32, (OWNERS // 2, WIDTH), 1) < BUCKET
    rows, kinds = rows[...], kinds[...]
    out[pl.ds(0, OWNERS // 2, stride=2), :] = jnp.where(first, rows, pltpu.roll(kinds, BUCKET, 1))
    out[pl.ds(1, OWNERS // 2, stride=2), :] = jnp.where(first, pltpu.roll(rows, BUCKET, 1), kinds)


def request(rows, kinds):
    return call(
        request_body,
        "request",
        [(shape(OWNERS, I32), VMEM)],
        [VMEM] * 2,
        [],
        WHOLE,
        moved=100_000,
    )(rows.reshape(-1, WIDTH), kinds.reshape(-1, WIDTH))[0]


def gather_tails_body(
    wanted_in, table_in, relations_in, out, factors_out, wanted, table, relations, rows, factors, weighted, in_sems, sems
):
    arrivals, copies = Copies(in_sems), Copies(sems)
    arrivals.start(wanted_in, wanted)
    arrivals.start(relations_in, relations)
    last = arrivals.start(table_in, table)
    for copy in arrivals.all[:2]:
        copy.wait()

    def factor(b, i):
        row = wanted[b * LINE + BUCKET + i]
        factors[pl.ds(b * BUCKET + i, 1), :] = relations[pl.ds(row, 1), :]

    for k in range(4):
        if k == 0:

            @pl.loop(0, OWNERS // 4)
            def _(b):
                for i in range(BUCKET):
                    factor(b, i)

            last.wait()

        @pl.loop(k * OWNERS // 4, (k + 1) * OWNERS // 4)
        def _(b):
            for i in range(BUCKET):
                rows[pl.ds(b * BUCKET + i, 1), :] = table[pl.ds(wanted[b * LINE + i], 1), :]
                if k > 0:
                    factor(b, i)

        part = pl.ds(k * SLOTS // 4, SLOTS // 4)
        weighted[part, :] = (factors[part, :] * rows[part, :].astype(BF16).astype(F32)).astype(BF16)
        copies.start(weighted.at[part], out.at[part])
        copies.start(factors.at[part], factors_out.at[part])
    copies.wait()


def gather_tails(wanted, table, relations):
    return call(
        gather_tails_body,
        "gather_tails",
        [
            (shape(SLOTS, BF16), HBM),
            (shape(SLOTS, F32), HBM),
        ],
        [HBM] * 3,
        [pltpu.SMEM(wanted.shape, I32), TABLE, pltpu.VMEM(relations.shape, F32), TABLE, TABLE]
        + [pltpu.VMEM((SLOTS, WIDTH), BF16), pltpu.SemaphoreType.DMA((3,)), pltpu.SemaphoreType.DMA((8,))],
        WORDS_STAY,
        flops=10_000_000_000,
        moved=20_000_000,
    )(wanted, table, relations)


def gather_own_body(place, src, table, out, rows, held, sems):
    copies = Copies(sems)
    head_rows(place, src, table, rows, (0,))
    held[...] = rows[...].astype(BF16)
    copies.start(held, out)
    copies.wait()


def gather_own(place, src, table):
    return call(
        gather_own_body,
        "gather_own",
        [(shape(EDGES, BF16), HBM)],
        [SMEM, SMEM, VMEM],
        [
            pltpu.VMEM((EDGES, WIDTH), F32),
            pltpu.VMEM((EDGES, WIDTH), BF16),
            pltpu.SemaphoreType.DMA((1,)),
        ],
        WHOLE,
        flops=3_000_000_000,
        moved=3_000_000,
    )(place, src, table)[0]


def edge_scores_body(
    settings_in, weighted_in, h0, n0, dr, vr, dl, vl, wr, wl, pulled_out, own, right, left, *rest
):
    settings, weighted, heads, corrupt, grad_scores, pulled, o, r, l, in_sems, sems = rest
    span = [slice(s * WIDTH, (s + 1) * WIDTH) for s in range(COLS)]
    arrivals, copies = Copies(in_sems), Copies(sems)
    for_masks = arrivals.start(settings_in, settings)

    def fetch(source, begin, target, row, s, n):
        return arrivals.start(source.at[pl.ds(begin, n)], target.at[pl.ds(row, n), pl.ds(s * WIDTH, WIDTH)])

    buckets = BLOCK // PART
    blocks = [pl.ds(k * buckets, buckets) for k in range(EDGES // BLOCK)]
    for_scores = [
        fetch(n0, 0, corrupt, 0, 0, NEG_PAD),
        fetch(vr, HALF, corrupt, 0, 1, HALF),
        fetch(dr, EDGES, corrupt, HALF, 1, HALF),
        fetch(wr, HALF, corrupt, 0, 2, HALF),
        fetch(wl, HALF, corrupt, HALF, 2, HALF),
        fetch(dl, EDGES, corrupt, 0, 3, HALF),
        fetch(vl, HALF, corrupt, HALF, 3, HALF),
    ]
    for_weights = [arrivals.start(weighted_in.at[at], weighted.at[at]) for at in blocks]
    for_heads = [
        fetch(h0, 0, heads, 0, 0, EDGES),
        fetch(dr, 0, heads, 0, 1, EDGES),
        fetch(wr, 0, heads, 0, 2, HALF),
        fetch(wl, 0, heads, HALF, 2, HALF),
        fetch(dl, 0, heads, 0, 3, EDGES),
    ]
    for_masks.wait()
    place = settings[0, BUCKETS_END]
    owner = [(place + COLS - s) & (COLS - 1) for s in range(COLS)]
    for copy in for_scores:
        copy.wait()

    def send(values, at, where, second):
        n = values.shape[0]
        via, via_out = (l, left) if second else (r, right)
        for s, held, out, begins in ((2, via, via_out, where), (1, l, left, at), (3, r, right, at), (0, o, own, at)):
            held[begins : begins + n, :] = values[:, span[s]]
            copies.start(held.at[pl.ds(begins, n)], out.at[pl.ds(begins, n)])

    negatives = corrupt[...]
    slot = lax.broadcasted_iota(I32, (PART, 1), 0) + place * PART
    whole = []
    for k in range(EDGES // BLOCK):
        rows = slice(k * BLOCK, (k + 1) * BLOCK)
        live = jnp.concatenate(
            [(slot < settings[0, b]).astype(F32) for b in range(k * buckets, (k + 1) * buckets)], axis=0
        )
        for_weights[k].wait()
        wk = jnp.concatenate(
            [weighted[k * buckets : (k + 1) * buckets, owner[s]].reshape(BLOCK, WIDTH) for s in range(COLS)],
            axis=1,
        )
        whole.append(wk)
        scores = lax.dot_general(wk, negatives, (((1,), (1,)), ((), ())), preferred_element_type=F32)
        if k == 0:
            for copy in for_heads:
                copy.wait()
        wf, hf = wk.astype(F32), heads[rows, :].astype(F32)
        positive = jnp.sum(hf * wf, axis=1, keepdims=True)
        grad_positive = -live * jax.nn.sigmoid(-positive)
        grad = (live * jax.nn.sigmoid(scores) * (1.0 / NEG)).astype(BF16)
        grad_scores[rows, :] = grad
        total = jnp.dot(grad, negatives, preferred_element_type=F32) + grad_positive * hf
        total = total.astype(BF16)
        at = blocks[k]
        for s in range(COLS):
            pulled[at, owner[s]] = total[:, span[s]].reshape(buckets, PART, WIDTH)
        copies.start(pulled.at[at], pulled_out.at[at])
        send((grad_positive * wf).astype(BF16), k * BLOCK, DIRECT + k * BLOCK % HALF, k * BLOCK >= HALF)
    weights = jnp.concatenate(whole, axis=0)
    for k in range(NEG_PAD // BLOCK):
        total = lax.dot_general(
            grad_scores[:, k * BLOCK : (k + 1) * BLOCK],
            weights,
            (((0,), (0,)), ((), ())),
            preferred_element_type=F32,
        )
        send(
            total.astype(BF16),
            EDGES + k * BLOCK,
            DIRECT + HALF + k * BLOCK % HALF,
            k * BLOCK >= HALF,
        )
    copies.wait()


def edge_scores(settings, weighted, pieces):
    whole = (OWNERS, COLS, PART, WIDTH)
    sizes = (DIRECT, DIRECT + 2 * HALF, DIRECT + 2 * HALF)
    return call(
        edge_scores_body,
        "edge_scores",
        [(jax.ShapeDtypeStruct(whole, BF16), HBM)] + [(shape(n, BF16), HBM) for n in sizes],
        [HBM] * 10,
        [
            pltpu.SMEM(settings.shape, I32),
            pltpu.VMEM(whole, BF16),
            pltpu.VMEM((EDGES, FULL), BF16),
            pltpu.VMEM((NEG_PAD, FULL), BF16),
            pltpu.VMEM((EDGES, NEG_PAD), BF16),
            pltpu.VMEM(whole, BF16),
        ]
        + [pltpu.VMEM((n, WIDTH), BF16) for n in sizes]
        + [pltpu.SemaphoreType.DMA((17,)), pltpu.SemaphoreType.DMA((36,))],
        WHOLE,
        flops=3_200_000_000,
        moved=8_000_000,
    )(settings, weighted, *pieces)


def begin(tables):
    for table in tables:
        table[...] = jnp.zeros((SLOTS, WIDTH), F32)


def finish(tables):
    total = tables[0][...]
    for table in tables[1:]:
        total += table[...]
    tables[0][...] = total


def scatter_near_body(settings_in, src_in, g0, g1, g3, out, settings, src, b0, b1, b3, r0, r1, r3, sems, *tables):
    tables = (out,) + tables
    copies = Copies(sems)
    copies.start(settings_in, settings)
    copies.start(src_in, src)
    for source, target in ((g0, b0), (g1, b1), (g3, b3)):
        copies.start(source.at[pl.ds(0, EDGES)], target)
    begin(tables)
    copies.wait()
    col = settings[0, BUCKETS_END]
    for source, target in ((b0, r0), (b1, r1), (b3, r3)):
        target[...] = source[...].astype(F32)

    @pl.loop(0, OWNERS)
    def _(b):
        for i in range(PART):
            for s, rows in ((0, r0), (1, r1), (3, r3)):
                base = b * BUCKET + ((col + s) & (COLS - 1)) * PART
                into = tables[(i * 3 + s) % CHAINS]
                into[pl.ds(src[base + i], 1), :] += rows[pl.ds(b * PART + i, 1), :]

    finish(tables)


def scatter_near(settings, src, g0, g1, g3):
    return call(
        scatter_near_body,
        "scatter_near",
        [(shape(SLOTS, F32), VMEM)],
        [HBM] * 5,
        [pltpu.SMEM(settings.shape, I32), pltpu.SMEM(src.shape, I32)]
        + [pltpu.VMEM((EDGES, WIDTH), BF16)] * 3
        + [pltpu.VMEM((EDGES, WIDTH), F32)] * 3
        + [pltpu.SemaphoreType.DMA((5,))]
        + [TABLE] * (CHAINS - 1),
        WHOLE,
        flops=10_000_000_000,
        moved=20_000_000,
    )(settings, src, g0, g1, g3)[0]


def scatter_far_body(
    settings_in, src_in, neg_in, start, g0, g1, g3, wr, wl, out, settings, src, neg, b0, b1, b3, br, bl, rr, rl, corrupt, sems, *tables
):
    tables = (out,) + tables
    copies = Copies(sems)
    for source, target in ((settings_in, settings), (src_in, src), (neg_in, neg)):
        copies.start(source, target)
    copies.start(wr, br)
    copies.start(wl, bl)
    for source, target in ((g0, b0), (g1, b1), (g3, b3)):
        copies.start(source.at[pl.ds(EDGES, NEG_PAD)], target)
    copies.start(start, out)
    begin(tables[1:])
    copies.wait()
    col = settings[0, BUCKETS_END]
    rr[...] = br[0:HALF, :].astype(F32)
    rl[...] = bl[0:HALF, :].astype(F32)
    near = b0[...].astype(F32) + b1[...].astype(F32) + b3[...].astype(F32)
    corrupt[0:HALF, :] = near[0:HALF, :] + br[HALF:, :].astype(F32)
    corrupt[HALF:, :] = near[HALF:, :] + bl[HALF:, :].astype(F32)

    @pl.loop(0, OWNERS // 2)
    def _(b):
        for i in range(PART):
            for n, rows in enumerate((rr, rl)):
                base = (b + n * OWNERS // 2) * BUCKET + ((col + 2) & (COLS - 1)) * PART
                into = tables[(i * 2 + n) % CHAINS]
                into[pl.ds(src[base + i], 1), :] += rows[pl.ds(b * PART + i, 1), :]

    @pl.loop(0, NEG // 40)
    def _(g):
        for i in range(40):
            into = tables[i % CHAINS]
            into[pl.ds(neg[g * 40 + i], 1), :] += corrupt[pl.ds(g * 40 + i, 1), :]

    finish(tables)


def scatter_far(settings, src, neg, start, g0, g1, g3, wr, wl):
    return call(
        scatter_far_body,
        "scatter_far",
        [(shape(SLOTS, F32), VMEM)],
        [HBM] * 9,
        [pltpu.SMEM(settings.shape, I32), pltpu.SMEM(src.shape, I32), pltpu.SMEM(neg.shape, I32)]
        + [pltpu.VMEM((NEG_PAD, WIDTH), BF16)] * 5
        + [pltpu.VMEM((HALF, WIDTH), F32)] * 2
        + [pltpu.VMEM((NEG_PAD, WIDTH), F32), pltpu.SemaphoreType.DMA((9,))]
        + [TABLE] * (CHAINS - 1),
        WHOLE,
        flops=10_000_000_000,
        moved=20_000_000,
    )(settings, src, neg, start, g0, g1, g3, wr, wl)[0]


def scatter_tails_body(
    wanted_in, start, factors, pulled, out, squares, wanted, held, scale, rows, first, in_sems, *tables
):
    arrivals = Copies(in_sems)
    for_rows = arrivals.start(wanted_in, wanted)
    parts = [pl.ds(k * SLOTS // 4, SLOTS // 4) for k in range(4)]
    needed = [
        [arrivals.start(source.at[part], target.at[part]) for source, target in ((pulled, held), (factors, scale))]
        for part in parts
    ]
    last = arrivals.start(start, first)
    begin(tables)
    for_rows.wait()
    for k, part in enumerate(parts):
        for copy in needed[k]:
            copy.wait()
        rows[part, :] = scale[part, :] * held[part, :].astype(F32)

        @pl.loop(k * OWNERS // 4, (k + 1) * OWNERS // 4)
        def _(b):
            for i in range(BUCKET):
                into = tables[i % CHAINS]
                into[pl.ds(wanted[b * BUCKET + i], 1), :] += rows[pl.ds(b * BUCKET + i, 1), :]

    last.wait()
    ones = jnp.ones((16, 2 * WIDTH), BF16)
    for k, part in enumerate(parts):
        total = first[part, :]
        for table in tables:
            total += table[part, :]
        out[part, :] = total
        square = total * total
        high = square.astype(BF16)
        low = (square - high.astype(F32)).astype(BF16)
        sums = lax.dot_general(
            ones, jnp.concatenate([high, low], axis=1), (((1,), (1,)), ((), ())), preferred_element_type=F32
        )
        for n in range(SLOTS // 4 // WIDTH):
            line = k * SLOTS // 4 // WIDTH + n
            squares[line : line + 1, :] = sums[0:1, n * WIDTH : (n + 1) * WIDTH]


def scatter_tails(wanted, start, factors, pulled):
    return call(
        scatter_tails_body,
        "scatter_tails",
        [(shape(SLOTS, F32), VMEM), (shape(SLOTS // WIDTH, F32), VMEM)],
        [HBM] * 4,
        [pltpu.SMEM((SLOTS,), I32), pltpu.VMEM((SLOTS, WIDTH), BF16), TABLE, TABLE, TABLE]
        + [pltpu.SemaphoreType.DMA((10,))]
        + [TABLE] * CHAINS,
        WHOLE,
        moved=30_000_000,
    )(wanted, start, factors, pulled)


def stage_body(table, gradient, table_out, step_out):
    table_out[...] = table[...]
    step_out[...] = gradient[...] * learning_rate


def stage(table, gradient):
    return call(
        stage_body,
        "stage",
        [(shape(SLOTS, F32), VMEM)] * 2,
        [VMEM] * 2,
        [],
        12 * 1024,
        moved=8_000_000,
    )(table, gradient)


def pass_on_body(g1, g3, out_r, out_l, r, l, in_sems, sems):
    arrivals, copies = Copies(in_sems), Copies(sems)
    arrivals.start(g3.at[pl.ds(DIRECT, 2 * HALF)], r)
    arrivals.start(g1.at[pl.ds(DIRECT, 2 * HALF)], l)
    arrivals.wait()
    copies.start(r, out_r)
    copies.start(l, out_l)
    copies.wait()


def pass_on(g1, g3):
    return call(
        pass_on_body,
        "pass_on",
        [(shape(2 * HALF, BF16), HBM)] * 2,
        [HBM] * 2,
        [pltpu.VMEM((2 * HALF, WIDTH), BF16)] * 2 + [pltpu.SemaphoreType.DMA((2,))] * 2,
        moved=1_000_000,
    )(g1, g3)


def shifted(x, s):
    return lax.ppermute(x, "col", [(i, (i + s) % COLS) for i in range(COLS)])


def shards(
    embeddings, adagrad_state, relations, src_rows, dst_rows, rel_ids, bucket_counts, neg_rows
):
    axes = ("dom", "col")
    place = lax.axis_index("col").astype(I32).reshape(1)
    settings = jnp.concatenate([bucket_counts, jnp.broadcast_to(place, bucket_counts.shape)], axis=1)

    def sent(x):
        return lax.all_to_all(
            x.reshape(OWNERS * COLS, PART, WIDTH), axes, split_axis=0, concat_axis=0, tiled=True
        )

    words = request(dst_rows, rel_ids)
    wanted = lax.all_to_all(words, "dom", split_axis=0, concat_axis=0, tiled=True)
    via_r, via_l, negatives = gather_far(place, src_rows, neg_rows, embeddings)
    vr, vl = shifted(via_r, 1), shifted(via_l, -1)
    weighted, factors = gather_tails(wanted.reshape(-1), embeddings, relations)
    weighted = sent(weighted).reshape(OWNERS, COLS, PART, WIDTH)
    after, factors, vr, vl = lax.optimization_barrier((negatives, factors, vr, vl))
    right, left = gather_near(place, src_rows, embeddings, after)
    near_r, near_l = shifted(right, 1), shifted(left, -1)
    wr, wl = shifted(vr, 1), shifted(vl, -1)
    own_rows, wr, wl = lax.optimization_barrier((src_rows, wr, wl))
    heads = gather_own(place, own_rows, embeddings)
    pieces = [heads, after, near_r, vr, near_l, vl, wr, wl]
    pulled, own, right, left = edge_scores(settings, weighted, pieces)
    pulled = sent(pulled).reshape(SLOTS, WIDTH)
    from_left, from_right = shifted(right, 1), shifted(left, -1)
    on_r, on_l = pass_on(from_right, from_left)
    far_a, far_b = shifted(on_r, 1), shifted(on_l, -1)
    gradient = scatter_near(settings, src_rows, own, from_right, from_left)
    gradient = scatter_far(settings, src_rows, neg_rows, gradient, own, from_right, from_left, far_a, far_b)
    gradient, squares = scatter_tails(
        wanted[:, :BUCKET].reshape(-1), gradient, factors, pulled
    )

    table, step = stage(embeddings, gradient)
    squares = (squares + shifted(squares, 2)) + (shifted(squares, 1) + shifted(squares, 3))
    new_state = adagrad_state + squares.reshape(-1) / FULL
    new_embeddings = table - step / jnp.sqrt(new_state)[:, None]
    return (new_embeddings, new_state)


def solution(mesh):
    placed = (
        P("dom", "col"),
        P("dom"),
        P(None, "col"),
        P("dom"),
        P("dom"),
        P("dom"),
        P("dom", None),
        P("dom"),
    )
    return jax.shard_map(
        shards, mesh=mesh, in_specs=placed, out_specs=(P("dom", "col"), P("dom")), check_vma=False
    )
```

```python
import jax
import jax.numpy as jnp
from jax import lax
from jax.experimental import pallas as pl
from jax.experimental.pallas import tpu as pltpu
from jax.sharding import PartitionSpec as P

learning_rate = 0.3
OWNERS = 64
COLS = 4
PART = 16
BUCKET = COLS * PART
SLOTS = OWNERS * BUCKET
EDGES = OWNERS * PART
WIDTH = 128
FULL = COLS * WIDTH
NEG = 1000
NEG_PAD = 1024
DIRECT = EDGES + NEG_PAD
BUCKETS_END = OWNERS
HALF = 512
BLOCK = 256
CHAINS = 8
WHOLE = 65_300
WORDS_STAY = 54_528

F32, BF16, I32 = jnp.float32, jnp.bfloat16, jnp.int32
SMEM = pl.BlockSpec(memory_space=pltpu.SMEM)
VMEM = pl.BlockSpec(memory_space=pltpu.VMEM)
HBM = pl.BlockSpec(memory_space=pltpu.HBM)
TABLE = pltpu.VMEM((SLOTS, WIDTH), F32)


def call(body, name, outs, ins, scratch, kib=WHOLE, flops=0, moved=0):
    return pl.pallas_call(
        body,
        out_shape=[shape for shape, _ in outs],
        in_specs=ins,
        out_specs=[spec for _, spec in outs],
        scratch_shapes=scratch,
        compiler_params=pltpu.CompilerParams(vmem_limit_bytes=kib * 1024),
        cost_estimate=pl.CostEstimate(flops=flops, bytes_accessed=moved, transcendentals=0),
        name=name,
    )


def shape(rows, dtype, width=WIDTH):
    return jax.ShapeDtypeStruct((rows, width), dtype)


def rows_at(start, count):
    return pl.ds(start, count)


class Copies:
    def __init__(self, sems):
        self.sems, self.all = sems, []

    def start(self, source, target):
        self.all.append(pltpu.make_async_copy(source, target, self.sems.at[len(self.all)]))
        self.all[-1].start()
        return self.all[-1]

    def wait(self):
        for copy in self.all:
            copy.wait()


def head_rows(place, src, table, rows, pieces):
    @pl.loop(0, OWNERS)
    def _(b):
        for n, s in enumerate(pieces):
            base = b * BUCKET + ((place[0] + s) & (COLS - 1)) * PART
            for i in range(PART):
                rows[pl.ds(n * EDGES + b * PART + i, 1), :] = table[pl.ds(src[base + i], 1), :]


def gather_far_body(place, src, neg, table, via_r, via_l, corrupt_out, first_out, second_out, rows, corrupt, rounded, vr, vl, sems):
    copies = Copies(sems)

    @pl.loop(0, NEG // 40)
    def _(g):
        for i in range(40):
            corrupt[pl.ds(g * 40 + i, 1), :] = table[pl.ds(neg[g * 40 + i], 1), :]

    corrupt[NEG:NEG_PAD, :] = jnp.zeros((NEG_PAD - NEG, WIDTH), F32)
    rounded[...] = corrupt[...].astype(BF16)
    copies.start(rounded, corrupt_out)
    copies.start(rounded.at[pl.ds(0, HALF)], first_out)
    copies.start(rounded.at[pl.ds(HALF, HALF)], second_out)
    head_rows(place, src, table, rows, (2,))
    for held, out, part in ((vr, via_r, slice(0, HALF)), (vl, via_l, slice(HALF, 2 * HALF))):
        held[0:HALF, :] = rows[part, :].astype(BF16)
        held[HALF:, :] = rounded[part, :]
        copies.start(held, out)
    copies.wait()


def gather_far(place, src, neg, table):
    return call(
        gather_far_body,
        "gather_far",
        [(shape(2 * HALF, BF16), HBM)] * 3 + [(shape(HALF, BF16), HBM)] * 2,
        [SMEM, SMEM, SMEM, VMEM],
        [pltpu.VMEM((EDGES, WIDTH), F32), pltpu.VMEM((NEG_PAD, WIDTH), F32)]
        + [pltpu.VMEM((2 * HALF, WIDTH), BF16)] * 3
        + [pltpu.SemaphoreType.DMA((5,))],
        WHOLE,
        moved=10_000_000,
    )(place, src, neg, table)


def gather_near_body(place, src, table, right, left, rows, r, l, sems):
    copies = Copies(sems)
    head_rows(place, src, table, rows, (1, 3))
    r[...] = rows[0:EDGES, :].astype(BF16)
    copies.start(r, right)
    l[...] = rows[EDGES : 2 * EDGES, :].astype(BF16)
    copies.start(l, left)
    copies.wait()


def gather_near(place, src, table):
    return call(
        gather_near_body,
        "gather_near",
        [(shape(EDGES, BF16), HBM)] * 2,
        [SMEM, SMEM, VMEM],
        [pltpu.VMEM((2 * EDGES, WIDTH), F32)]
        + [pltpu.VMEM((EDGES, WIDTH), BF16)] * 2
        + [pltpu.SemaphoreType.DMA((2,))],
        WHOLE,
        flops=17_000_000_000,
        moved=20_000_000,
    )(place, src, table)


LINE = 2 * BUCKET


def request_body(rows, kinds, out):
    first = lax.broadcasted_iota(I32, (OWNERS // 2, WIDTH), 1) < BUCKET
    rows, kinds = rows[...], kinds[...]
    out[pl.ds(0, OWNERS // 2, stride=2), :] = jnp.where(first, rows, pltpu.roll(kinds, BUCKET, 1))
    out[pl.ds(1, OWNERS // 2, stride=2), :] = jnp.where(first, pltpu.roll(rows, BUCKET, 1), kinds)


def request(rows, kinds):
    return call(
        request_body,
        "request",
        [(shape(OWNERS, I32), VMEM)],
        [VMEM] * 2,
        [],
        WHOLE,
        moved=100_000,
    )(rows.reshape(-1, WIDTH), kinds.reshape(-1, WIDTH))[0]


def gather_tails_body(
    wanted_in, table_in, relations_in, out, factors_out, wanted, table, relations, rows, factors, weighted, in_sems, sems
):
    arrivals, copies = Copies(in_sems), Copies(sems)
    arrivals.start(wanted_in, wanted)
    arrivals.start(relations_in, relations)
    last = arrivals.start(table_in, table)
    for copy in arrivals.all[:2]:
        copy.wait()

    def factor(b, i):
        row = wanted[b * LINE + BUCKET + i]
        factors[pl.ds(b * BUCKET + i, 1), :] = relations[pl.ds(row, 1), :]

    for k in range(4):
        if k == 0:

            @pl.loop(0, OWNERS // 4)
            def _(b):
                for i in range(BUCKET):
                    factor(b, i)

            last.wait()

        @pl.loop(k * OWNERS // 4, (k + 1) * OWNERS // 4)
        def _(b):
            for i in range(BUCKET):
                rows[pl.ds(b * BUCKET + i, 1), :] = table[pl.ds(wanted[b * LINE + i], 1), :]
                if k > 0:
                    factor(b, i)

        part = pl.ds(k * SLOTS // 4, SLOTS // 4)
        weighted[part, :] = (factors[part, :] * rows[part, :].astype(BF16).astype(F32)).astype(BF16)
        copies.start(weighted.at[part], out.at[part])
        copies.start(factors.at[part], factors_out.at[part])
    copies.wait()


def gather_tails(wanted, table, relations):
    return call(
        gather_tails_body,
        "gather_tails",
        [
            (shape(SLOTS, BF16), HBM),
            (shape(SLOTS, F32), HBM),
        ],
        [HBM] * 3,
        [pltpu.SMEM(wanted.shape, I32), TABLE, pltpu.VMEM(relations.shape, F32), TABLE, TABLE]
        + [pltpu.VMEM((SLOTS, WIDTH), BF16), pltpu.SemaphoreType.DMA((3,)), pltpu.SemaphoreType.DMA((8,))],
        WORDS_STAY,
        flops=10_000_000_000,
        moved=20_000_000,
    )(wanted, table, relations)


def gather_own_body(place, src, table, out, rows, held, sems):
    copies = Copies(sems)
    head_rows(place, src, table, rows, (0,))
    held[...] = rows[...].astype(BF16)
    copies.start(held, out)
    copies.wait()


def gather_own(place, src, table):
    return call(
        gather_own_body,
        "gather_own",
        [(shape(EDGES, BF16), HBM)],
        [SMEM, SMEM, VMEM],
        [
            pltpu.VMEM((EDGES, WIDTH), F32),
            pltpu.VMEM((EDGES, WIDTH), BF16),
            pltpu.SemaphoreType.DMA((1,)),
        ],
        WHOLE,
        flops=3_000_000_000,
        moved=3_000_000,
    )(place, src, table)[0]


def edge_scores_body(
    settings_in, weighted_in, h0, n0, dr, nr, vr, dl, nl, vl, wr, wl, pulled_out, own, right, left, *rest
):
    settings, weighted, heads, corrupt, grad_scores, pulled, o, r, l, in_sems, sems = rest
    span = [slice(s * WIDTH, (s + 1) * WIDTH) for s in range(COLS)]
    arrivals, copies = Copies(in_sems), Copies(sems)
    for_masks = arrivals.start(settings_in, settings)

    def fetch(source, begin, target, row, s, n):
        return arrivals.start(source.at[pl.ds(begin, n)], target.at[pl.ds(row, n), pl.ds(s * WIDTH, WIDTH)])

    buckets = BLOCK // PART
    blocks = [pl.ds(k * buckets, buckets) for k in range(EDGES // BLOCK)]
    for_scores = [
        fetch(n0, 0, corrupt, 0, 0, NEG_PAD),
        fetch(vr, HALF, corrupt, 0, 1, HALF),
        fetch(nr, 0, corrupt, HALF, 1, HALF),
        fetch(wr, HALF, corrupt, 0, 2, HALF),
        fetch(wl, HALF, corrupt, HALF, 2, HALF),
        fetch(nl, 0, corrupt, 0, 3, HALF),
        fetch(vl, HALF, corrupt, HALF, 3, HALF),
    ]
    for_weights = [arrivals.start(weighted_in.at[at], weighted.at[at]) for at in blocks]
    for_heads = [
        fetch(h0, 0, heads, 0, 0, EDGES),
        fetch(dr, 0, heads, 0, 1, EDGES),
        fetch(wr, 0, heads, 0, 2, HALF),
        fetch(wl, 0, heads, HALF, 2, HALF),
        fetch(dl, 0, heads, 0, 3, EDGES),
    ]
    for_masks.wait()
    place = settings[0, BUCKETS_END]
    owner = [(place + COLS - s) & (COLS - 1) for s in range(COLS)]
    for copy in for_scores:
        copy.wait()

    def send(values, at, where, second):
        n = values.shape[0]
        via, via_out = (l, left) if second else (r, right)
        for s, held, out, begins in ((2, via, via_out, where), (1, l, left, at), (3, r, right, at), (0, o, own, at)):
            held[begins : begins + n, :] = values[:, span[s]]
            copies.start(held.at[pl.ds(begins, n)], out.at[pl.ds(begins, n)])

    negatives = corrupt[...]
    slot = lax.broadcasted_iota(I32, (PART, 1), 0) + place * PART
    whole = []
    for k in range(EDGES // BLOCK):
        rows = slice(k * BLOCK, (k + 1) * BLOCK)
        live = jnp.concatenate(
            [(slot < settings[0, b]).astype(F32) for b in range(k * buckets, (k + 1) * buckets)], axis=0
        )
        for_weights[k].wait()
        wk = jnp.concatenate(
            [weighted[k * buckets : (k + 1) * buckets, owner[s]].reshape(BLOCK, WIDTH) for s in range(COLS)],
            axis=1,
        )
        whole.append(wk)
        scores = lax.dot_general(wk, negatives, (((1,), (1,)), ((), ())), preferred_element_type=F32)
        if k == 0:
            for copy in for_heads:
                copy.wait()
        wf, hf = wk.astype(F32), heads[rows, :].astype(F32)
        positive = jnp.sum(hf * wf, axis=1, keepdims=True)
        grad_positive = -live * jax.nn.sigmoid(-positive)
        grad = (live * jax.nn.sigmoid(scores) * (1.0 / NEG)).astype(BF16)
        grad_scores[rows, :] = grad
        total = jnp.dot(grad, negatives, preferred_element_type=F32) + grad_positive * hf
        total = total.astype(BF16)
        at = blocks[k]
        for s in range(COLS):
            pulled[at, owner[s]] = total[:, span[s]].reshape(buckets, PART, WIDTH)
        copies.start(pulled.at[at], pulled_out.at[at])
        send((grad_positive * wf).astype(BF16), k * BLOCK, DIRECT + k * BLOCK % HALF, k * BLOCK >= HALF)
    weights = jnp.concatenate(whole, axis=0)
    for k in range(NEG_PAD // BLOCK):
        total = lax.dot_general(
            grad_scores[:, k * BLOCK : (k + 1) * BLOCK],
            weights,
            (((0,), (0,)), ((), ())),
            preferred_element_type=F32,
        )
        send(
            total.astype(BF16),
            EDGES + k * BLOCK,
            DIRECT + HALF + k * BLOCK % HALF,
            k * BLOCK >= HALF,
        )
    copies.wait()


def edge_scores(settings, weighted, pieces):
    whole = (OWNERS, COLS, PART, WIDTH)
    sizes = (DIRECT, DIRECT + 2 * HALF, DIRECT + 2 * HALF)
    return call(
        edge_scores_body,
        "edge_scores",
        [(jax.ShapeDtypeStruct(whole, BF16), HBM)] + [(shape(n, BF16), HBM) for n in sizes],
        [HBM] * 12,
        [
            pltpu.SMEM(settings.shape, I32),
            pltpu.VMEM(whole, BF16),
            pltpu.VMEM((EDGES, FULL), BF16),
            pltpu.VMEM((NEG_PAD, FULL), BF16),
            pltpu.VMEM((EDGES, NEG_PAD), BF16),
            pltpu.VMEM(whole, BF16),
        ]
        + [pltpu.VMEM((n, WIDTH), BF16) for n in sizes]
        + [pltpu.SemaphoreType.DMA((17,)), pltpu.SemaphoreType.DMA((36,))],
        WHOLE,
        flops=3_200_000_000,
        moved=8_000_000,
    )(settings, weighted, *pieces)


def begin(tables):
    for table in tables:
        table[...] = jnp.zeros((SLOTS, WIDTH), F32)


def finish(tables):
    total = tables[0][...]
    for table in tables[1:]:
        total += table[...]
    tables[0][...] = total


def scatter_near_body(settings_in, src_in, g0, g1, g3, out, settings, src, b0, b1, b3, r0, r1, r3, sems, *tables):
    tables = (out,) + tables
    copies = Copies(sems)
    copies.start(settings_in, settings)
    copies.start(src_in, src)
    for source, target in ((g0, b0), (g1, b1), (g3, b3)):
        copies.start(source.at[pl.ds(0, EDGES)], target)
    begin(tables)
    copies.wait()
    col = settings[0, BUCKETS_END]
    for source, target in ((b0, r0), (b1, r1), (b3, r3)):
        target[...] = source[...].astype(F32)

    @pl.loop(0, OWNERS)
    def _(b):
        for i in range(PART):
            for s, rows in ((0, r0), (1, r1), (3, r3)):
                base = b * BUCKET + ((col + s) & (COLS - 1)) * PART
                into = tables[(i * 3 + s) % CHAINS]
                into[pl.ds(src[base + i], 1), :] += rows[pl.ds(b * PART + i, 1), :]

    finish(tables)


def scatter_near(settings, src, g0, g1, g3):
    return call(
        scatter_near_body,
        "scatter_near",
        [(shape(SLOTS, F32), VMEM)],
        [HBM] * 5,
        [pltpu.SMEM(settings.shape, I32), pltpu.SMEM(src.shape, I32)]
        + [pltpu.VMEM((EDGES, WIDTH), BF16)] * 3
        + [pltpu.VMEM((EDGES, WIDTH), F32)] * 3
        + [pltpu.SemaphoreType.DMA((5,))]
        + [TABLE] * (CHAINS - 1),
        WHOLE,
        flops=10_000_000_000,
        moved=20_000_000,
    )(settings, src, g0, g1, g3)[0]


def scatter_far_body(
    settings_in, src_in, neg_in, start, g0, g1, g3, wr, wl, out, settings, src, neg, b0, b1, b3, br, bl, rr, rl, corrupt, sems, *tables
):
    tables = (out,) + tables
    copies = Copies(sems)
    for source, target in ((settings_in, settings), (src_in, src), (neg_in, neg)):
        copies.start(source, target)
    copies.start(wr, br)
    copies.start(wl, bl)
    for source, target in ((g0, b0), (g1, b1), (g3, b3)):
        copies.start(source.at[pl.ds(EDGES, NEG_PAD)], target)
    copies.start(start, out)
    begin(tables[1:])
    copies.wait()
    col = settings[0, BUCKETS_END]
    rr[...] = br[0:HALF, :].astype(F32)
    rl[...] = bl[0:HALF, :].astype(F32)
    near = b0[...].astype(F32) + b1[...].astype(F32) + b3[...].astype(F32)
    corrupt[0:HALF, :] = near[0:HALF, :] + br[HALF:, :].astype(F32)
    corrupt[HALF:, :] = near[HALF:, :] + bl[HALF:, :].astype(F32)

    @pl.loop(0, OWNERS // 2)
    def _(b):
        for i in range(PART):
            for n, rows in enumerate((rr, rl)):
                base = (b + n * OWNERS // 2) * BUCKET + ((col + 2) & (COLS - 1)) * PART
                into = tables[(i * 2 + n) % CHAINS]
                into[pl.ds(src[base + i], 1), :] += rows[pl.ds(b * PART + i, 1), :]

    @pl.loop(0, NEG // 40)
    def _(g):
        for i in range(40):
            into = tables[i % CHAINS]
            into[pl.ds(neg[g * 40 + i], 1), :] += corrupt[pl.ds(g * 40 + i, 1), :]

    finish(tables)


def scatter_far(settings, src, neg, start, g0, g1, g3, wr, wl):
    return call(
        scatter_far_body,
        "scatter_far",
        [(shape(SLOTS, F32), VMEM)],
        [HBM] * 9,
        [pltpu.SMEM(settings.shape, I32), pltpu.SMEM(src.shape, I32), pltpu.SMEM(neg.shape, I32)]
        + [pltpu.VMEM((NEG_PAD, WIDTH), BF16)] * 5
        + [pltpu.VMEM((HALF, WIDTH), F32)] * 2
        + [pltpu.VMEM((NEG_PAD, WIDTH), F32), pltpu.SemaphoreType.DMA((9,))]
        + [TABLE] * (CHAINS - 1),
        WHOLE,
        flops=10_000_000_000,
        moved=20_000_000,
    )(settings, src, neg, start, g0, g1, g3, wr, wl)[0]


def scatter_tails_body(
    wanted_in, start, factors, pulled, out, squares, wanted, held, scale, rows, first, in_sems, *tables
):
    arrivals = Copies(in_sems)
    for_rows = arrivals.start(wanted_in, wanted)
    parts = [pl.ds(k * SLOTS // 4, SLOTS // 4) for k in range(4)]
    needed = [
        [arrivals.start(source.at[part], target.at[part]) for source, target in ((pulled, held), (factors, scale))]
        for part in parts
    ]
    last = arrivals.start(start, first)
    begin(tables)
    for_rows.wait()
    for k, part in enumerate(parts):
        for copy in needed[k]:
            copy.wait()
        rows[part, :] = scale[part, :] * held[part, :].astype(F32)

        @pl.loop(k * OWNERS // 4, (k + 1) * OWNERS // 4)
        def _(b):
            for i in range(BUCKET):
                into = tables[i % CHAINS]
                into[pl.ds(wanted[b * BUCKET + i], 1), :] += rows[pl.ds(b * BUCKET + i, 1), :]

    last.wait()
    ones = jnp.ones((16, 2 * WIDTH), BF16)
    for k, part in enumerate(parts):
        total = first[part, :]
        for table in tables:
            total += table[part, :]
        out[part, :] = total
        square = total * total
        high = square.astype(BF16)
        low = (square - high.astype(F32)).astype(BF16)
        sums = lax.dot_general(
            ones, jnp.concatenate([high, low], axis=1), (((1,), (1,)), ((), ())), preferred_element_type=F32
        )
        for n in range(SLOTS // 4 // WIDTH):
            line = k * SLOTS // 4 // WIDTH + n
            squares[line : line + 1, :] = sums[0:1, n * WIDTH : (n + 1) * WIDTH]


def scatter_tails(wanted, start, factors, pulled):
    return call(
        scatter_tails_body,
        "scatter_tails",
        [(shape(SLOTS, F32), VMEM), (shape(SLOTS // WIDTH, F32), VMEM)],
        [HBM] * 4,
        [pltpu.SMEM((SLOTS,), I32), pltpu.VMEM((SLOTS, WIDTH), BF16), TABLE, TABLE, TABLE]
        + [pltpu.SemaphoreType.DMA((10,))]
        + [TABLE] * CHAINS,
        WHOLE,
        moved=30_000_000,
    )(wanted, start, factors, pulled)


def stage_body(table, gradient, table_out, step_out):
    table_out[...] = table[...]
    step_out[...] = gradient[...] * learning_rate


def stage(table, gradient):
    return call(
        stage_body,
        "stage",
        [(shape(SLOTS, F32), VMEM)] * 2,
        [VMEM] * 2,
        [],
        12 * 1024,
        moved=8_000_000,
    )(table, gradient)


def pass_on_body(g1, g3, out_r, out_l, r, l, in_sems, sems):
    arrivals, copies = Copies(in_sems), Copies(sems)
    arrivals.start(g3.at[pl.ds(DIRECT, 2 * HALF)], r)
    arrivals.start(g1.at[pl.ds(DIRECT, 2 * HALF)], l)
    arrivals.wait()
    copies.start(r, out_r)
    copies.start(l, out_l)
    copies.wait()


def pass_on(g1, g3):
    return call(
        pass_on_body,
        "pass_on",
        [(shape(2 * HALF, BF16), HBM)] * 2,
        [HBM] * 2,
        [pltpu.VMEM((2 * HALF, WIDTH), BF16)] * 2 + [pltpu.SemaphoreType.DMA((2,))] * 2,
        moved=1_000_000,
    )(g1, g3)


def shifted(x, s):
    return lax.ppermute(x, "col", [(i, (i + s) % COLS) for i in range(COLS)])


def shards(
    embeddings, adagrad_state, relations, src_rows, dst_rows, rel_ids, bucket_counts, neg_rows
):
    axes = ("dom", "col")
    place = lax.axis_index("col").astype(I32).reshape(1)
    settings = jnp.concatenate([bucket_counts, jnp.broadcast_to(place, bucket_counts.shape)], axis=1)

    def sent(x):
        return lax.all_to_all(
            x.reshape(OWNERS * COLS, PART, WIDTH), axes, split_axis=0, concat_axis=0, tiled=True
        )

    words = request(dst_rows, rel_ids)
    wanted = lax.all_to_all(words, "dom", split_axis=0, concat_axis=0, tiled=True)
    via_r, via_l, negatives, first, second = gather_far(place, src_rows, neg_rows, embeddings)
    vr, vl = shifted(via_r, 1), shifted(via_l, -1)
    weighted, factors = gather_tails(wanted.reshape(-1), embeddings, relations)
    weighted = sent(weighted).reshape(OWNERS, COLS, PART, WIDTH)
    after, first, second, near_rows, factors, vr, vl = lax.optimization_barrier(
        (negatives, first, second, src_rows, factors, vr, vl)
    )
    nr, nl = shifted(second, 1), shifted(first, -1)
    wr, wl = shifted(vr, 1), shifted(vl, -1)
    right, left = gather_near(place, near_rows, embeddings)
    near_r, near_l = shifted(right, 1), shifted(left, -1)
    own_rows, nr, nl, wr, wl = lax.optimization_barrier((src_rows, nr, nl, wr, wl))
    heads = gather_own(place, own_rows, embeddings)
    pieces = [heads, after, near_r, nr, vr, near_l, nl, vl, wr, wl]
    pulled, own, right, left = edge_scores(settings, weighted, pieces)
    pulled = sent(pulled).reshape(SLOTS, WIDTH)
    from_left, from_right = shifted(right, 1), shifted(left, -1)
    on_r, on_l = pass_on(from_right, from_left)
    far_a, far_b = shifted(on_r, 1), shifted(on_l, -1)
    gradient = scatter_near(settings, src_rows, own, from_right, from_left)
    gradient = scatter_far(settings, src_rows, neg_rows, gradient, own, from_right, from_left, far_a, far_b)
    gradient, squares = scatter_tails(
        wanted[:, :BUCKET].reshape(-1), gradient, factors, pulled
    )

    table, step = stage(embeddings, gradient)
    squares = (squares + shifted(squares, 2)) + (shifted(squares, 1) + shifted(squares, 3))
    new_state = adagrad_state + squares.reshape(-1) / FULL
    new_embeddings = table - step / jnp.sqrt(new_state)[:, None]
    return (new_embeddings, new_state)


def solution(mesh):
    placed = (
        P("dom", "col"),
        P("dom"),
        P(None, "col"),
        P("dom"),
        P("dom"),
        P("dom"),
        P("dom", None),
        P("dom"),
    )
    return jax.shard_map(
        shards, mesh=mesh, in_specs=placed, out_specs=(P("dom", "col"), P("dom")), check_vma=False
    )
```
